256 devices in a mesh: dp: 16 (over x_lo, y, core), feat: 16 (over x_hi, z).
Axes of the slice: x: 4 (x_hi: 2, x_lo: 2; x = x_hi * 2 + x_lo), y: 4, z: 8, core: 2. Of those that a mesh axis runs over, the one named last changes fastest.
Arguments:
- view_a: bfloat16 [2048, 16384], P('dp', 'feat'), may hold values from -240 to 240
- view_b: bfloat16 [2048, 16384], P('dp', 'feat'), may hold values from -240 to 240
Outputs:
- grad_a: bfloat16 [2048, 16384], P('dp', 'feat')
- grad_b: bfloat16 [2048, 16384], P('dp', 'feat')
The draws below stay inside these ranges and needn't reach their ends.
All inputs are finite; a program needn't handle non-finite values.
Results may differ from the reference program's by a relative error of at most 0.028.
Values may be sent and summed in bfloat16 or wider, within the bound.
No kernel may reach another device: no remote copies, remote signals or barrier semaphores. Data moves between devices by JAX's collectives and lax.ppermute only.
A program may use at most 128 MiB of HBM per device.

```python
import jax
import jax.numpy as jnp
from jax import lax

FEATS = 16384
BATCH = 2048


def shared_parts(key):
    key_base, key_common, key_load, key_sign, key_scale = jax.random.split(key, 5)
    base = jnp.clip(jax.random.normal(key_base, (BATCH, FEATS), jnp.float32), -4.0, 4.0)
    common = jnp.clip(jax.random.normal(key_common, (BATCH,), jnp.float32), -4.0, 4.0)
    loading = jax.random.uniform(key_load, (FEATS,), jnp.float32, 0.5, 1.5)
    loading = loading * jnp.where(jax.random.bernoulli(key_sign, 0.5, (FEATS,)), 1.0, -1.0)
    position = jnp.arange(BATCH, dtype=jnp.float32) / max(BATCH - 1, 1)
    row_scale = (1.0 + 2.0 * position) * jnp.exp(jax.random.uniform(key_scale, (BATCH,), jnp.float32, 0.0, 1.19))
    return (base + 0.07 * common[:, None] * loading[None, :], row_scale)


def make_view(key, salt):
    mixed, row_scale = shared_parts(key)
    key = jax.random.fold_in(key, salt)
    key_noise, key_col, key_offset = jax.random.split(key, 3)
    noise = jnp.clip(jax.random.normal(key_noise, (BATCH, FEATS), jnp.float32), -4.0, 4.0)
    col_scale = jnp.exp(jax.random.uniform(key_col, (FEATS,), jnp.float32, -0.69, 1.38))
    offset = jax.random.uniform(key_offset, (FEATS,), jnp.float32, -2.0, 2.0)
    value = (mixed + 0.35 * noise) * row_scale[:, None] * col_scale[None, :] + offset[None, :]
    return value.astype(jnp.bfloat16)


def draw_view_a(key, part):
    return make_view(key, 11)


def draw_view_b(key, part):
    return make_view(key, 12)


def setup_inputs(seed: int = 0) -> dict:
    streams_of = jax.random.split(jax.random.key(seed), 3)
    return {
        "view_a": draw_view_a(jax.random.fold_in(streams_of[2], 71), 0),
        "view_b": draw_view_b(jax.random.fold_in(streams_of[2], 71), 0),
    }


off_weight = 0.0051
epsilon = 1e-05

def normalize(view):
    values = view.astype(jnp.float32)
    col_mean = lax.optimization_barrier(jnp.mean(values, 0))
    centered = values - col_mean
    spread = jnp.sqrt(lax.optimization_barrier(jnp.mean(centered * centered, 0)) + epsilon)
    return ((centered / spread).astype(jnp.bfloat16), spread)

def backward(upward, normed, spread):
    normal_f = normed.astype(jnp.float32)
    first_mean = lax.optimization_barrier(jnp.mean(upward, 0))
    second_mean = lax.optimization_barrier(jnp.mean(upward * normal_f, 0))
    return ((upward - first_mean - normal_f * second_mean) / spread).astype(jnp.bfloat16)

def reference(view_a, view_b):
    normed_a, spread_a = normalize(view_a)
    normed_b, spread_b = normalize(view_b)
    block_count = 16
    block_width = FEATS // block_count

    def one_block(carry, block_id):
        offset = block_id * block_width
        section = lax.dynamic_slice_in_dim(normed_a, offset, block_width, 1)
        corr = lax.dot_general(section, normed_b, (((0,), (0,)), ((), ())), preferred_element_type=jnp.float32) * (1.0 / BATCH)
        row_ids = offset + lax.broadcasted_iota(jnp.int32, (block_width, FEATS), 0)
        col_ids = lax.broadcasted_iota(jnp.int32, (block_width, FEATS), 1)
        corr_grad = jnp.where(row_ids == col_ids, 2.0 * (corr - 1.0), 2.0 * off_weight * corr).astype(jnp.bfloat16)
        up_block = lax.dot_general(normed_b, corr_grad, (((1,), (1,)), ((), ())), preferred_element_type=jnp.float32)
        carry = carry + jnp.dot(section, corr_grad, preferred_element_type=jnp.float32)
        return (carry, up_block)
    start_carry = jnp.zeros((BATCH, FEATS), jnp.float32)
    up_b, up_blocks = lax.scan(one_block, start_carry, jnp.arange(block_count, dtype=jnp.int32))
    up_a = jnp.transpose(up_blocks, (1, 0, 2)).reshape(BATCH, FEATS)
    return (backward(up_a, normed_a, spread_a), backward(up_b, normed_b, spread_b))
```

```python
import functools

import jax
import jax.numpy as jnp
from jax import lax
from jax.experimental import pallas as pl
from jax.experimental.pallas import tpu as pltpu
from jax.sharding import PartitionSpec as P

off_weight = 0.0051
epsilon = 1e-05
f32 = jnp.float32
bf16 = jnp.bfloat16

X_LO, Y, CORES = 2, 4, 2


def dp_perm(move):
    def index(x, y, c):
        return (x * Y + y) * CORES + c

    return [
        (index(x, y, c), index(*move(x, y, c)))
        for x in range(X_LO)
        for y in range(Y)
        for c in range(CORES)
    ]


TO_CORE = dp_perm(lambda x, y, c: (x, y, 1 - c))
TO_X = dp_perm(lambda x, y, c: (1 - x, y, c))
TO_UP = dp_perm(lambda x, y, c: (x, (y + 1) % Y, c))
TO_DOWN = dp_perm(lambda x, y, c: (x, (y - 1) % Y, c))


def call(body, outs, *args, flops=0):
    def size(s):
        return s.size * s.dtype.itemsize

    return pl.pallas_call(
        body,
        out_shape=outs,
        in_specs=[pl.BlockSpec(memory_space=pltpu.VMEM)] * len(args),
        out_specs=jax.tree.map(lambda _: pl.BlockSpec(memory_space=pltpu.VMEM), outs),
        compiler_params=pltpu.CompilerParams(vmem_limit_bytes=40 * 2**20),
        cost_estimate=pl.CostEstimate(
            flops=flops,
            bytes_accessed=sum(size(a) for a in args) + sum(size(o) for o in jax.tree.leaves(outs)),
            transcendentals=0,
        ),
    )(*args)


def shape(*dims, dtype=f32):
    return jax.ShapeDtypeStruct(dims, dtype)


def gather_chips(view):
    half = view.shape[1] // 2
    from_down = lax.ppermute(view, "dp", TO_UP)
    from_up = lax.ppermute(view, "dp", TO_DOWN)
    from_x = lax.ppermute(view, "dp", TO_X)
    far_left = lax.ppermute(from_down[:, :half], "dp", TO_UP)
    far_right = lax.ppermute(from_up[:, half:], "dp", TO_DOWN)
    x_down = lax.ppermute(from_x, "dp", TO_UP)
    x_up = lax.ppermute(from_x, "dp", TO_DOWN)
    far = jnp.concatenate([far_left, far_right], 1)
    x_far = lax.ppermute(far, "dp", TO_X)
    return [view, from_down, from_up, from_x, far, x_down, x_up, x_far]


def moments_body(*refs):
    pieces, out = refs[:-1], refs[-1]
    count = sum(p.shape[0] for p in pieces)
    total = sum(jnp.sum(p[...].astype(f32), 0, keepdims=True) for p in pieces)
    mean = total / count
    square = 0.0
    for p in pieces:
        centered = p[...].astype(f32) - mean
        square = square + jnp.sum(centered * centered, 0, keepdims=True)
    out[0:1, :] = mean
    out[1:2, :] = square


def gram_body(batch, *refs):
    *pieces, sib, own_m, sib_m, normed, normed_sib, spread_out, gram = refs
    mean = 0.5 * (own_m[0:1, :] + sib_m[0:1, :])
    gap = own_m[0:1, :] - sib_m[0:1, :]
    square = own_m[1:2, :] + sib_m[1:2, :] + gap * gap * (batch / 4)
    spread = jnp.sqrt(square / batch + epsilon)
    spread_out[...] = spread
    rows = sib.shape[0]
    normed_sib[...] = ((sib[...].astype(f32) - mean) / spread).astype(bf16)
    for i, p in enumerate(pieces):
        normed[i * rows : (i + 1) * rows, :] = ((p[...].astype(f32) - mean) / spread).astype(bf16)
    groups, part = gram.shape[0], gram.shape[1]
    nt = (((1,), (1,)), ((), ()))
    for i in range(len(pieces)):
        block = normed[i * rows : (i + 1) * rows, :]
        top = lax.dot_general(normed[0:rows, :], block, nt, preferred_element_type=f32)
        low = lax.dot_general(normed_sib[...], block, nt, preferred_element_type=f32)
        gram[0 : groups // 2, :, i * rows : (i + 1) * rows] = top.astype(bf16).reshape(
            groups // 2, part, rows
        )
        gram[groups // 2 :, :, i * rows : (i + 1) * rows] = low.astype(bf16).reshape(
            groups // 2, part, rows
        )


def diag_body(a, b, out):
    total = 0.0
    step = 128
    for i in range(a.shape[0] // step):
        s = slice(i * step, (i + 1) * step)
        total = total + jnp.sum(a[s, :].astype(f32) * b[s, :].astype(f32), 0, keepdims=True)
    out[...] = total


def reduce_body(parts, out):
    total = parts[0].astype(f32)
    for i in range(1, parts.shape[0]):
        total = total + parts[i].astype(f32)
    total = total.astype(bf16)
    for i in range(out.shape[0]):
        out[i] = total


def apply_body(scale, gram, normed, own, other):
    rows = own.shape[0]
    own[...] = scale * jnp.dot(gram[0:rows, :], normed[...], preferred_element_type=f32)
    other[...] = scale * jnp.dot(gram[rows:, :], normed[...], preferred_element_type=f32)


def upward_body(batch, own, recv, normed_other, normed_self, diag_own, diag_sib, up_out, sums):
    rows = own.shape[0]
    corr = (diag_own[...] + diag_sib[...]) / batch
    diag = 2.0 * (corr - 1.0) - 2.0 * off_weight * corr
    up = own[...] + recv[...] + normed_other[0:rows, :].astype(f32) * diag
    up_out[...] = up
    first = jnp.sum(up, 0, keepdims=True)
    second = jnp.sum(up * normed_self[0:rows, :].astype(f32), 0, keepdims=True)
    for i in range(sums.shape[0]):
        sums[i, 0:1, :] = first
        sums[i, 1:2, :] = second


def final_body(batch, up, normed_self, sums, spread, out):
    rows = up.shape[0]
    total = sums[0]
    for i in range(1, sums.shape[0]):
        total = total + sums[i]
    total = total / batch
    normal = normed_self[0:rows, :].astype(f32)
    out[...] = ((up[...] - total[0:1, :] - normal * total[1:2, :]) / spread[...]).astype(bf16)


def on_device(view_a, view_b):
    rows, cols = view_a.shape
    dp_count = lax.axis_size("dp")
    feat_count = lax.axis_size("feat")
    batch = rows * dp_count
    half = batch // CORES
    part = CORES * rows // feat_count
    scale = 2.0 * off_weight / batch

    def prepare(view):
        pieces = gather_chips(view)
        sib = lax.ppermute(view, "dp", TO_CORE)
        moments = call(moments_body, shape(2, cols), *pieces)
        moments_sib = lax.ppermute(moments, "dp", TO_CORE)
        return call(
            functools.partial(gram_body, batch),
            (
                shape(half, cols, dtype=bf16),
                shape(rows, cols, dtype=bf16),
                shape(1, cols),
                shape(feat_count, part, half, dtype=bf16),
            ),
            *pieces,
            sib,
            moments,
            moments_sib,
            flops=2 * CORES * rows * half * cols,
        )

    def reduce(gram):
        parts = lax.all_to_all(gram, "feat", 0, 0)
        total = call(reduce_body, shape(feat_count, part, half, dtype=bf16), parts)
        whole = lax.all_to_all(total, "feat", 0, 0)
        return whole.reshape(CORES * rows, half)

    def upward(gram, normed_self, normed_other, diag, diag_sib):
        own, other = call(
            functools.partial(apply_body, scale),
            (shape(rows, cols), shape(rows, cols)),
            gram,
            normed_self,
            flops=2 * CORES * rows * half * cols,
        )
        recv = lax.ppermute(other, "dp", TO_CORE)
        return call(
            functools.partial(upward_body, batch),
            (shape(rows, cols), shape(dp_count, 2, cols)),
            own,
            recv,
            normed_other,
            normed_self,
            diag,
            diag_sib,
        )

    def finish(up, sums, normed_self, spread):
        sums = lax.all_to_all(sums, "dp", 0, 0)
        return call(
            functools.partial(final_body, batch),
            shape(rows, cols, dtype=bf16),
            up,
            normed_self,
            sums,
            spread,
        )

    normed_a, _, spread_a, part_a = prepare(view_a)
    gram_a = reduce(part_a)
    normed_b, _, spread_b, part_b = prepare(view_b)
    gram_b = reduce(part_b)
    diag = call(diag_body, shape(1, cols), normed_a, normed_b)
    diag_sib = lax.ppermute(diag, "dp", TO_CORE)
    up_b, sums_b = upward(gram_a, normed_b, normed_a, diag, diag_sib)
    grad_b = finish(up_b, sums_b, normed_b, spread_b)
    up_a, sums_a = upward(gram_b, normed_a, normed_b, diag, diag_sib)
    grad_a = finish(up_a, sums_a, normed_a, spread_a)
    return (grad_a, grad_b)


def solution(mesh):
    spec = P("dp", "feat")
    return jax.shard_map(
        on_device, mesh=mesh, in_specs=(spec, spec), out_specs=(spec, spec), check_vma=False
    )
```

```python
import functools

import jax
import jax.numpy as jnp
from jax import lax
from jax.experimental import pallas as pl
from jax.experimental.pallas import tpu as pltpu
from jax.sharding import PartitionSpec as P

off_weight = 0.0051
epsilon = 1e-05
f32 = jnp.float32
bf16 = jnp.bfloat16

X_LO, Y, CORES = 2, 4, 2


def dp_perm(move):
    def index(x, y, c):
        return (x * Y + y) * CORES + c

    return [
        (index(x, y, c), index(*move(x, y, c)))
        for x in range(X_LO)
        for y in range(Y)
        for c in range(CORES)
    ]


TO_CORE = dp_perm(lambda x, y, c: (x, y, 1 - c))
TO_X = dp_perm(lambda x, y, c: (1 - x, y, c))
TO_UP = dp_perm(lambda x, y, c: (x, (y + 1) % Y, c))
TO_DOWN = dp_perm(lambda x, y, c: (x, (y - 1) % Y, c))


def call(body, outs, *args, flops=0):
    def size(s):
        return s.size * s.dtype.itemsize

    return pl.pallas_call(
        body,
        out_shape=outs,
        in_specs=[pl.BlockSpec(memory_space=pltpu.VMEM)] * len(args),
        out_specs=jax.tree.map(lambda _: pl.BlockSpec(memory_space=pltpu.VMEM), outs),
        compiler_params=pltpu.CompilerParams(vmem_limit_bytes=24 * 2**20),
        cost_estimate=pl.CostEstimate(
            flops=flops,
            bytes_accessed=sum(size(a) for a in args) + sum(size(o) for o in jax.tree.leaves(outs)),
            transcendentals=0,
        ),
    )(*args)


def shape(*dims, dtype=f32):
    return jax.ShapeDtypeStruct(dims, dtype)


def gather_chips(view):
    half = view.shape[1] // 2
    from_down = lax.ppermute(view, "dp", TO_UP)
    from_up = lax.ppermute(view, "dp", TO_DOWN)
    from_x = lax.ppermute(view, "dp", TO_X)
    far_left = lax.ppermute(from_down[:, :half], "dp", TO_UP)
    far_right = lax.ppermute(from_up[:, half:], "dp", TO_DOWN)
    x_down = lax.ppermute(from_x, "dp", TO_UP)
    x_up = lax.ppermute(from_x, "dp", TO_DOWN)
    far = jnp.concatenate([far_left, far_right], 1)
    x_far = lax.ppermute(far, "dp", TO_X)
    return [view, from_down, from_up, from_x, far, x_down, x_up, x_far]


def moments_body(*refs):
    pieces, out = refs[:-1], refs[-1]
    for v in range(2):
        view = pieces[v * len(pieces) // 2 : (v + 1) * len(pieces) // 2]
        count = sum(p.shape[0] for p in view)
        total = sum(jnp.sum(p[...].astype(f32), 0, keepdims=True) for p in view)
        mean = total / count
        square = 0.0
        for p in view:
            centered = p[...].astype(f32) - mean
            square = square + jnp.sum(centered * centered, 0, keepdims=True)
        out[2 * v : 2 * v + 1, :] = mean
        out[2 * v + 1 : 2 * v + 2, :] = square


def gram_body(batch, *refs):
    *pieces, own_m, sib_m, normed_a, normed_b, spread_out, diag, gram = refs
    rows = pieces[0].shape[0]
    groups, part = gram.shape[0], gram.shape[2]
    nt = (((1,), (1,)), ((), ()))
    for v, normed in enumerate((normed_a, normed_b)):
        view = pieces[v * len(pieces) // 2 : (v + 1) * len(pieces) // 2]
        m, q = slice(2 * v, 2 * v + 1), slice(2 * v + 1, 2 * v + 2)
        mean = 0.5 * (own_m[m, :] + sib_m[m, :])
        gap = own_m[m, :] - sib_m[m, :]
        square = own_m[q, :] + sib_m[q, :] + gap * gap * (batch / 4)
        spread = jnp.sqrt(square / batch + epsilon)
        spread_out[v : v + 1, :] = spread
        for i, p in enumerate(view):
            normed[i * rows : (i + 1) * rows, :] = ((p[...].astype(f32) - mean) / spread).astype(bf16)
        sib = normed[len(view) * rows - rows :, :]
        for i in range(len(view) - 1):
            block = normed[i * rows : (i + 1) * rows, :]
            top = lax.dot_general(normed[0:rows, :], block, nt, preferred_element_type=f32)
            low = lax.dot_general(sib, block, nt, preferred_element_type=f32)
            c = slice(i * rows, (i + 1) * rows)
            gram[0 : groups // 2, v, :, c] = top.astype(bf16).reshape(groups // 2, part, rows)
            gram[groups // 2 :, v, :, c] = low.astype(bf16).reshape(groups // 2, part, rows)
    total = 0.0
    for i in range(len(pieces) // 2 - 1):
        c = slice(i * rows, (i + 1) * rows)
        total = total + jnp.sum(
            normed_a[c, :].astype(f32) * normed_b[c, :].astype(f32), 0, keepdims=True
        )
    diag[...] = total


def reduce_body(parts, out):
    total = parts[0].astype(f32)
    for i in range(1, parts.shape[0]):
        total = total + parts[i].astype(f32)
    total = total.astype(bf16)
    for i in range(out.shape[0]):
        out[i] = total


def apply_body(scale, gram, normed_a, normed_b, own, other):
    groups = gram.shape[0]
    half, rows = gram.shape[3], own.shape[1]
    for v, normed in enumerate((normed_b, normed_a)):
        for part, out in enumerate((own, other)):
            block = gram[part * groups // 2 : (part + 1) * groups // 2, v].reshape(rows, half)
            out[v] = scale * jnp.dot(block, normed[0:half, :], preferred_element_type=f32)


def upward_body(batch, own, recv, normed_a, normed_b, diag_own, diag_sib, up_out, sums):
    rows = own.shape[1]
    corr = (diag_own[...] + diag_sib[...]) / batch
    diag = 2.0 * (corr - 1.0) - 2.0 * off_weight * corr
    for v, (other, same) in enumerate(((normed_a, normed_b), (normed_b, normed_a))):
        up = own[v] + recv[v] + other[0:rows, :].astype(f32) * diag
        up_out[v] = up
        first = jnp.sum(up, 0, keepdims=True)
        second = jnp.sum(up * same[0:rows, :].astype(f32), 0, keepdims=True)
        for i in range(sums.shape[0]):
            sums[i, 2 * v : 2 * v + 1, :] = first
            sums[i, 2 * v + 1 : 2 * v + 2, :] = second


def final_body(batch, up, normed_a, normed_b, sums, spread, grad_a, grad_b):
    rows = up.shape[1]
    total = sums[0]
    for i in range(1, sums.shape[0]):
        total = total + sums[i]
    total = total / batch
    for v, (same, out) in enumerate(((normed_b, grad_b), (normed_a, grad_a))):
        normal = same[0:rows, :].astype(f32)
        first, second = total[2 * v : 2 * v + 1, :], total[2 * v + 1 : 2 * v + 2, :]
        divisor = spread[1 - v : 2 - v, :]
        out[...] = ((up[v] - first - normal * second) / divisor).astype(bf16)


def on_device(view_a, view_b):
    rows, cols = view_a.shape
    dp_count = lax.axis_size("dp")
    feat_count = lax.axis_size("feat")
    batch = rows * dp_count
    half = batch // CORES
    part = CORES * rows // feat_count
    scale = 2.0 * off_weight / batch
    work = 2 * 2 * CORES * rows * half * cols

    pieces_a, pieces_b = gather_chips(view_a), gather_chips(view_b)
    sib_a = lax.ppermute(view_a, "dp", TO_CORE)
    sib_b = lax.ppermute(view_b, "dp", TO_CORE)
    moments = call(moments_body, shape(4, cols), *pieces_a, *pieces_b)
    moments_sib = lax.ppermute(moments, "dp", TO_CORE)
    normed_a, normed_b, spread, diag, gram = call(
        functools.partial(gram_body, batch),
        (
            shape(half + rows, cols, dtype=bf16),
            shape(half + rows, cols, dtype=bf16),
            shape(2, cols),
            shape(1, cols),
            shape(feat_count, 2, part, half, dtype=bf16),
        ),
        *pieces_a,
        sib_a,
        *pieces_b,
        sib_b,
        moments,
        moments_sib,
        flops=work,
    )
    diag_sib = lax.ppermute(diag, "dp", TO_CORE)
    parts = lax.all_to_all(gram, "feat", 0, 0)
    total = call(reduce_body, shape(feat_count, 2, part, half, dtype=bf16), parts)
    whole = lax.all_to_all(total, "feat", 0, 0)
    own, other = call(
        functools.partial(apply_body, scale),
        (shape(2, rows, cols), shape(2, rows, cols)),
        whole,
        normed_a,
        normed_b,
        flops=work,
    )
    recv = lax.ppermute(other, "dp", TO_CORE)
    up, sums = call(
        functools.partial(upward_body, batch),
        (shape(2, rows, cols), shape(dp_count, 4, cols)),
        own,
        recv,
        normed_a,
        normed_b,
        diag,
        diag_sib,
    )
    sums = lax.all_to_all(sums, "dp", 0, 0)
    return call(
        functools.partial(final_body, batch),
        (shape(rows, cols, dtype=bf16), shape(rows, cols, dtype=bf16)),
        up,
        normed_a,
        normed_b,
        sums,
        spread,
    )


def solution(mesh):
    spec = P("dp", "feat")
    return jax.shard_map(
        on_device, mesh=mesh, in_specs=(spec, spec), out_specs=(spec, spec), check_vma=False
    )
```

```python
import functools

import jax
import jax.numpy as jnp
from jax import lax
from jax.experimental import pallas as pl
from jax.experimental.pallas import tpu as pltpu
from jax.sharding import PartitionSpec as P

off_weight = 0.0051
epsilon = 1e-05
f32 = jnp.float32
bf16 = jnp.bfloat16

X_LO, Y, CORES = 2, 4, 2


def dp_perm(move):
    def index(x, y, c):
        return (x * Y + y) * CORES + c

    return [
        (index(x, y, c), index(*move(x, y, c)))
        for x in range(X_LO)
        for y in range(Y)
        for c in range(CORES)
    ]


TO_CORE = dp_perm(lambda x, y, c: (x, y, 1 - c))
TO_X = dp_perm(lambda x, y, c: (1 - x, y, c))
TO_UP = dp_perm(lambda x, y, c: (x, (y + 1) % Y, c))
TO_DOWN = dp_perm(lambda x, y, c: (x, (y - 1) % Y, c))


X_HI, Z = 2, 8
TO_X_HI = [(q, (q + Z) % (X_HI * Z)) for q in range(X_HI * Z)]


def z_shift(step):
    return [(h * Z + z, h * Z + (z + step) % Z) for h in range(X_HI) for z in range(Z)]


def send(x, to, axis="dp"):
    return lax.ppermute(x, axis, to)


def call(body, outs, *args, flops=0, scratch=()):
    def size(s):
        return s.size * s.dtype.itemsize

    return pl.pallas_call(
        body,
        out_shape=outs,
        in_specs=[pl.BlockSpec(memory_space=pltpu.VMEM)] * len(args),
        scratch_shapes=scratch,
        out_specs=jax.tree.map(lambda _: pl.BlockSpec(memory_space=pltpu.VMEM), outs),
        compiler_params=pltpu.CompilerParams(vmem_limit_bytes=16 * 2**20),
        cost_estimate=pl.CostEstimate(
            flops=flops,
            bytes_accessed=sum(size(a) for a in args) + sum(size(o) for o in jax.tree.leaves(outs)),
            transcendentals=0,
        ),
    )(*args)


def shape(*dims, dtype=f32):
    return jax.ShapeDtypeStruct(dims, dtype)


def moments_of(pieces):
    count = sum(p.shape[0] for p in pieces)
    total = sum(jnp.sum(p[...].astype(f32), 0, keepdims=True) for p in pieces)
    mean = total / count
    square = 0.0
    for p in pieces:
        centered = p[...].astype(f32) - mean
        square = square + jnp.sum(centered * centered, 0, keepdims=True)
    return count, mean, square


def early_moments_body(*refs):
    *pairs, far_a, far_b, out = refs
    for v, far in enumerate((far_a, far_b)):
        _, mean, square = moments_of([p.at[v] for p in pairs] + [far])
        out[2 * v : 2 * v + 1, :] = mean
        out[2 * v + 1 : 2 * v + 2, :] = square


def late_moments_body(early_count, early, far, out):
    for v in range(2):
        late_count, late_mean, late_square = moments_of([far.at[v]])
        mean = early[2 * v : 2 * v + 1, :]
        gap = late_mean - mean
        count = early_count + late_count
        out[2 * v : 2 * v + 1, :] = mean + gap * (late_count / count)
        out[2 * v + 1 : 2 * v + 2, :] = (
            early[2 * v + 1 : 2 * v + 2, :]
            + late_square
            + gap * gap * (early_count * late_count / count)
        )


def gram_body(batch, own_m, sib_m, sib, *refs):
    pairs, fars, outs = refs[:6], refs[6:9], refs[9:]
    lead, normed, spread_out, diag, mine, up_2, down_2, up_1, down_1, far_a, far_b, gram = outs
    rows, part = sib.shape[1], mine.shape[2]
    for v in range(2):
        m, q = slice(2 * v, 2 * v + 1), slice(2 * v + 1, 2 * v + 2)
        mean = 0.5 * (own_m[m, :] + sib_m[m, :])
        gap = own_m[m, :] - sib_m[m, :]
        square = own_m[q, :] + sib_m[q, :] + gap * gap * (batch / 4)
        spread = jnp.sqrt(square / batch + epsilon)
        spread_out[v : v + 1, :] = spread
        pieces = [p.at[v] for p in pairs] + [fars[v], fars[2].at[v]]
        for i, p in enumerate((pieces[0], sib.at[v])):
            r = slice(i * rows, (i + 1) * rows)
            lead[v, r, :] = ((p[...].astype(f32) - mean) / spread).astype(bf16)
        for i, p in enumerate(pieces):
            r = slice(i * rows, (i + 1) * rows)
            normed[v, r, :] = ((p[...].astype(f32) - mean) / spread).astype(bf16)
            block = lax.dot_general(
                lead[v], normed[v, r, :], (((1,), (1,)), ((), ())), preferred_element_type=f32
            )
            gram[v, :, r] = block.astype(bf16)
    z = lax.rem(lax.axis_index("feat"), Z)

    def store(ahead, v, out):
        start = lax.rem(z + ahead, Z) * part
        for h in range(X_HI):
            out[h] = gram[v, pl.ds(pl.multiple_of(start + h * rows, part), part), :]

    for v in range(2):
        store(0, v, mine.at[v])
        store(2, v, up_2.at[v])
        store(6, v, down_2.at[v])
        for i, (up, down) in enumerate(((3, 5), (1, 7))):
            store(up, v, up_1.at[i, v])
            store(down, v, down_1.at[i, v])
        store(4, v, (far_a, far_b)[v])
    total = 0.0
    for i in range(normed.shape[1] // rows):
        r = slice(i * rows, (i + 1) * rows)
        total = total + jnp.sum(
            normed[0, r, :].astype(f32) * normed[1, r, :].astype(f32), 0, keepdims=True
        )
    diag[...] = total


def fold_body(far_up, far_down, half_a, half_b, up_2, down_2, up_out, down_out):
    def plus(x, y, *z):
        total = x.astype(f32) + y.astype(f32)
        return (total + z[0].astype(f32) if z else total).astype(bf16)

    up_out[0] = plus(up_2[0], far_up[0, 0], half_a[...])
    up_out[1] = plus(up_2[1], far_up[0, 1])
    down_out[0] = plus(down_2[0], far_down[0, 0])
    down_out[1] = plus(down_2[1], far_down[0, 1], half_b[...])


def total_body(mine, near_up, near_down, far_up, far_down, out):
    total = mine[...].astype(f32) + near_up[1].astype(f32) + near_down[1].astype(f32)
    out[...] = (total + far_up[...].astype(f32) + far_down[...].astype(f32)).astype(bf16)


def add_body(a, b, out):
    out[...] = (a[...].astype(f32) + b[...].astype(f32)).astype(bf16)


def reduce_rows(mine, up_2, down_2, up_1, down_1, far_a, far_b):
    z = "feat"
    half_a = send(far_a, z_shift(2), z)
    half_b = send(far_b, z_shift(-2), z)
    from_down, from_up = send(up_1, z_shift(1), z), send(down_1, z_shift(-1), z)
    block = jax.ShapeDtypeStruct(mine.shape, bf16)
    up_2, down_2 = call(
        fold_body, (block, block), from_down, from_up, half_a, half_b, up_2, down_2
    )
    far_down, far_up = send(up_2, z_shift(2), z), send(down_2, z_shift(-2), z)
    total = call(total_body, block, mine, from_down, from_up, far_down, far_up)
    return call(add_body, block, total, send(total, TO_X_HI, z))


def spread_rows(block):
    z = "feat"
    from_1 = send(block, z_shift(1), z)
    from_7 = send(block, z_shift(-1), z)
    from_2 = send(block, z_shift(2), z)
    from_6 = send(block, z_shift(-2), z)
    from_3 = send(from_2, z_shift(1), z)
    from_5 = send(from_6, z_shift(-1), z)
    from_4a = send(from_2[0], z_shift(2), z)
    from_4b = send(from_6[1], z_shift(-2), z)
    return [block, from_1, from_2, from_3, from_5, from_6, from_7, from_4a, from_4b]


def apply_body(batch, scale, *refs):
    *blocks, from_4a, from_4b, normed, lead, diag_own, diag_sib, own, other, sums, gram = refs
    rows, part = own.shape[1], blocks[0].shape[2]
    z = lax.rem(lax.axis_index("feat"), Z)

    def load(back, v, block):
        start = lax.rem(z + Z - back, Z) * part
        for h in range(X_HI):
            gram[v, pl.ds(pl.multiple_of(start + h * rows, part), part), :] = block[h]

    for v in range(2):
        for back, block in zip((0, 1, 2, 3, 5, 6, 7), blocks):
            load(back, v, block.at[v])
        load(4, v, (from_4a, from_4b)[v])
    corr = (diag_own[...] + diag_sib[...]) / batch
    diag = 2.0 * (corr - 1.0) - 2.0 * off_weight * corr
    for v in range(2):
        first = second = 0.0
        for h, out in enumerate((own, other)):
            r = slice(h * rows, (h + 1) * rows)
            up = scale * jnp.dot(gram[1 - v, r, :], normed[v], preferred_element_type=f32)
            if h == 0:
                up = up + lead[1 - v, r, :].astype(f32) * diag
            out[v] = up
            first = first + jnp.sum(up, 0, keepdims=True)
            second = second + jnp.sum(up * lead[v, r, :].astype(f32), 0, keepdims=True)
        for i in range(sums.shape[0]):
            sums[i, 2 * v : 2 * v + 1, :] = first
            sums[i, 2 * v + 1 : 2 * v + 2, :] = second


def final_body(batch, own, recv, lead, sums, spread, grad_a, grad_b):
    rows = own.shape[1]
    total = sums[0]
    for i in range(1, sums.shape[0]):
        total = total + sums[i]
    total = total / batch
    for v, out in enumerate((grad_a, grad_b)):
        normal = lead[v, 0:rows, :].astype(f32)
        first, second = total[2 * v : 2 * v + 1, :], total[2 * v + 1 : 2 * v + 2, :]
        up = own[v] + recv[v]
        out[...] = ((up - first - normal * second) / spread[v : v + 1, :]).astype(bf16)


def on_device(view_a, view_b):
    rows, cols = view_a.shape
    dp_count = lax.axis_size("dp")
    feat_count = lax.axis_size("feat")
    batch = rows * dp_count
    half = batch // CORES
    part = CORES * rows // feat_count
    scale = 2.0 * off_weight / batch
    work = 2 * 2 * CORES * rows * half * cols

    views = jnp.stack([view_a, view_b])
    from_down, from_up, from_x = send(views, TO_UP), send(views, TO_DOWN), send(views, TO_X)
    sib = send(views, TO_CORE)
    far_a, far_b = send(from_down[0], TO_UP), send(from_up[1], TO_DOWN)
    x_down, x_up = send(from_x, TO_UP), send(from_x, TO_DOWN)
    x_far = send(jnp.stack([far_a, far_b]), TO_X)
    pairs = [views, from_down, from_up, from_x, x_down, x_up]
    early = call(early_moments_body, shape(4, cols), *pairs, far_a, far_b)
    moments = call(
        functools.partial(late_moments_body, half - rows), shape(4, cols), early, x_far
    )
    one = shape(X_HI, part, half, dtype=bf16)
    both = shape(2, *one.shape, dtype=bf16)
    four = shape(2, *both.shape, dtype=bf16)
    lead, normed, spread, diag, *chunks = call(
        functools.partial(gram_body, batch),
        (
            shape(2, CORES * rows, cols, dtype=bf16),
            shape(2, half, cols, dtype=bf16),
            shape(2, cols),
            shape(1, cols),
            both,
            both,
            both,
            four,
            four,
            one,
            one,
        ),
        moments,
        send(moments, TO_CORE),
        sib,
        *pairs,
        far_a,
        far_b,
        x_far,
        flops=work,
        scratch=[pltpu.VMEM((2, CORES * rows, half), bf16)],
    )
    diag_sib = send(diag, TO_CORE)
    blocks = spread_rows(reduce_rows(*chunks))
    own, other, sums = call(
        functools.partial(apply_body, batch, scale),
        (shape(2, rows, cols), shape(2, rows, cols), shape(dp_count, 4, cols)),
        *blocks,
        normed,
        lead,
        diag,
        diag_sib,
        flops=work,
        scratch=[pltpu.VMEM((2, CORES * rows, half), bf16)],
    )
    sums = lax.all_to_all(sums, "dp", 0, 0)
    return call(
        functools.partial(final_body, batch),
        (shape(rows, cols, dtype=bf16), shape(rows, cols, dtype=bf16)),
        own,
        send(other, TO_CORE),
        lead,
        sums,
        spread,
    )


def solution(mesh):
    spec = P("dp", "feat")
    return jax.shard_map(
        on_device, mesh=mesh, in_specs=(spec, spec), out_specs=(spec, spec), check_vma=False
    )
```

```python
import functools

import jax
import jax.numpy as jnp
from jax import lax
from jax.experimental import pallas as pl
from jax.experimental.pallas import tpu as pltpu
from jax.sharding import PartitionSpec as P

off_weight = 0.0051
epsilon = 1e-05
f32 = jnp.float32
bf16 = jnp.bfloat16

X_LO, Y, CORES = 2, 4, 2


def dp_perm(move):
    def index(x, y, c):
        return (x * Y + y) * CORES + c

    return [
        (index(x, y, c), index(*move(x, y, c)))
        for x in range(X_LO)
        for y in range(Y)
        for c in range(CORES)
    ]


TO_CORE = dp_perm(lambda x, y, c: (x, y, 1 - c))
TO_X = dp_perm(lambda x, y, c: (1 - x, y, c))
TO_UP = dp_perm(lambda x, y, c: (x, (y + 1) % Y, c))
TO_DOWN = dp_perm(lambda x, y, c: (x, (y - 1) % Y, c))


X_HI, Z = 2, 8
TO_X_HI = [(q, (q + Z) % (X_HI * Z)) for q in range(X_HI * Z)]


def z_shift(step):
    return [(h * Z + z, h * Z + (z + step) % Z) for h in range(X_HI) for z in range(Z)]


def send(x, to, axis="dp"):
    return lax.ppermute(x, axis, to)


def call(body, outs, *args, flops=0, scratch=()):
    def size(s):
        return s.size * s.dtype.itemsize

    return pl.pallas_call(
        body,
        out_shape=outs,
        in_specs=[pl.BlockSpec(memory_space=pltpu.VMEM)] * len(args),
        scratch_shapes=scratch,
        out_specs=jax.tree.map(lambda _: pl.BlockSpec(memory_space=pltpu.VMEM), outs),
        compiler_params=pltpu.CompilerParams(vmem_limit_bytes=16 * 2**20),
        cost_estimate=pl.CostEstimate(
            flops=flops,
            bytes_accessed=sum(size(a) for a in args) + sum(size(o) for o in jax.tree.leaves(outs)),
            transcendentals=0,
        ),
    )(*args)


def shape(*dims, dtype=f32):
    return jax.ShapeDtypeStruct(dims, dtype)


def moments_of(pieces_a, pieces_b):
    count = sum(p.shape[0] for p in pieces_a)
    mean_a = sum(jnp.sum(p[...].astype(f32), 0, keepdims=True) for p in pieces_a) / count
    mean_b = sum(jnp.sum(p[...].astype(f32), 0, keepdims=True) for p in pieces_b) / count
    square_a = square_b = product = 0.0
    for p, q in zip(pieces_a, pieces_b):
        a, b = p[...].astype(f32) - mean_a, q[...].astype(f32) - mean_b
        square_a = square_a + jnp.sum(a * a, 0, keepdims=True)
        square_b = square_b + jnp.sum(b * b, 0, keepdims=True)
        product = product + jnp.sum(a * b, 0, keepdims=True)
    return count, (mean_a, mean_b, square_a, square_b, product)


def merge(count, one, other_count, other):
    total = count + other_count
    gap_a, gap_b = other[0] - one[0], other[1] - one[1]
    weight = count * other_count / total
    return (
        one[0] + gap_a * (other_count / total),
        one[1] + gap_b * (other_count / total),
        one[2] + other[2] + gap_a * gap_a * weight,
        one[3] + other[3] + gap_b * gap_b * weight,
        one[4] + other[4] + gap_a * gap_b * weight,
    )


def put_rows(out, values):
    for i, value in enumerate(values):
        out[i : i + 1, :] = value


def get_rows(ref):
    return [ref[i : i + 1, :] for i in range(ref.shape[0])]


def early_moments_body(*refs):
    *pieces, out = refs
    single, stacked = pieces[:2], pieces[2:]
    _, moments = moments_of(
        [single[0], *(p.at[0] for p in stacked)], [single[1], *(p.at[1] for p in stacked)]
    )
    put_rows(out, moments)


def late_moments_body(early_count, early, *refs):
    *pairs, out = refs
    count, late = moments_of([p.at[0] for p in pairs], [p.at[1] for p in pairs])
    put_rows(out, merge(early_count, get_rows(early), count, late))


def gram_body(batch, own_m, sib_m, sib, *refs):
    *refs, lead, normed, stats, mine, up_2, down_2, up_1, down_1, far_a, far_b, gram = refs
    single, stacked = refs[:2], refs[2:]
    rows, part = sib.shape[1], mine.shape[2]
    mean_a, mean_b, square_a, square_b, product = merge(
        batch // 2, get_rows(own_m), batch // 2, get_rows(sib_m)
    )
    spreads = [jnp.sqrt(square / batch + epsilon) for square in (square_a, square_b)]
    corr = product / (batch * spreads[0] * spreads[1])
    put_rows(stats, (*spreads, 2.0 * (corr - 1.0) - 2.0 * off_weight * corr))
    for v, (mean, spread) in enumerate(zip((mean_a, mean_b), spreads)):
        view = [*(p.at[v] for p in stacked), single[v]]
        for i, p in enumerate((view[0], sib.at[v])):
            r = slice(i * rows, (i + 1) * rows)
            lead[v, r, :] = ((p[...].astype(f32) - mean) / spread).astype(bf16)
        for i, p in enumerate(view):
            r = slice(i * rows, (i + 1) * rows)
            normed[v, r, :] = ((p[...].astype(f32) - mean) / spread).astype(bf16)
            block = lax.dot_general(
                lead[v], normed[v, r, :], (((1,), (1,)), ((), ())), preferred_element_type=f32
            )
            gram[v, :, r] = block.astype(bf16)
    z = lax.rem(lax.axis_index("feat"), Z)

    def store(ahead, v, out):
        start = lax.rem(z + ahead, Z) * part
        for h in range(X_HI):
            out[h] = gram[v, pl.ds(pl.multiple_of(start + h * rows, part), part), :]

    for v in range(2):
        store(0, v, mine.at[v])
        store(2, v, up_2.at[v])
        store(6, v, down_2.at[v])
        for i, (up, down) in enumerate(((3, 5), (1, 7))):
            store(up, v, up_1.at[i, v])
            store(down, v, down_1.at[i, v])
        store(4, v, (far_a, far_b)[v])


def fold_body(far_up, far_down, half_a, half_b, up_2, down_2, up_out, down_out):
    def plus(x, y, *z):
        total = x.astype(f32) + y.astype(f32)
        return (total + z[0].astype(f32) if z else total).astype(bf16)

    up_out[0] = plus(up_2[0], far_up[0, 0], half_a[...])
    up_out[1] = plus(up_2[1], far_up[0, 1])
    down_out[0] = plus(down_2[0], far_down[0, 0])
    down_out[1] = plus(down_2[1], far_down[0, 1], half_b[...])


def total_body(mine, near_up, near_down, far_up, far_down, out):
    total = mine[...].astype(f32) + near_up[1].astype(f32) + near_down[1].astype(f32)
    out[...] = (total + far_up[...].astype(f32) + far_down[...].astype(f32)).astype(bf16)


def add_body(a, b, out):
    out[...] = (a[...].astype(f32) + b[...].astype(f32)).astype(bf16)


def reduce_rows(mine, up_2, down_2, up_1, down_1, far_a, far_b):
    z = "feat"
    half_a = send(far_a, z_shift(2), z)
    half_b = send(far_b, z_shift(-2), z)
    from_down, from_up = send(up_1, z_shift(1), z), send(down_1, z_shift(-1), z)
    block = jax.ShapeDtypeStruct(mine.shape, bf16)
    up_2, down_2 = call(
        fold_body, (block, block), from_down, from_up, half_a, half_b, up_2, down_2
    )
    far_down, far_up = send(up_2, z_shift(2), z), send(down_2, z_shift(-2), z)
    total = call(total_body, block, mine, from_down, from_up, far_down, far_up)
    return call(add_body, block, total, send(total, TO_X_HI, z))


def spread_rows(block):
    z = "feat"
    from_1 = send(block, z_shift(1), z)
    from_7 = send(block, z_shift(-1), z)
    from_2 = send(block, z_shift(2), z)
    from_6 = send(block, z_shift(-2), z)
    from_3 = send(from_2, z_shift(1), z)
    from_5 = send(from_6, z_shift(-1), z)
    from_4a = send(from_2[0], z_shift(2), z)
    from_4b = send(from_6[1], z_shift(-2), z)
    return [block, from_1, from_2, from_3, from_5, from_6, from_7, from_4a, from_4b]


def apply_body(scale, *refs):
    *blocks, from_4a, from_4b, normed, lead, stats, own, other, sums, gram = refs
    rows, part = own.shape[1], blocks[0].shape[2]
    z = lax.rem(lax.axis_index("feat"), Z)

    def load(back, v, block):
        start = lax.rem(z + Z - back, Z) * part
        for h in range(X_HI):
            gram[v, pl.ds(pl.multiple_of(start + h * rows, part), part), :] = block[h]

    for v in range(2):
        for back, block in zip((0, 1, 2, 3, 5, 6, 7), blocks):
            load(back, v, block.at[v])
        load(4, v, (from_4a, from_4b)[v])
    diag = stats[2:3, :]
    for v in range(2):
        first = second = 0.0
        for h, out in enumerate((own, other)):
            r = slice(h * rows, (h + 1) * rows)
            up = scale * jnp.dot(gram[1 - v, r, :], normed[v], preferred_element_type=f32)
            if h == 0:
                up = up + lead[1 - v, r, :].astype(f32) * diag
            out[v] = up
            first = first + jnp.sum(up, 0, keepdims=True)
            second = second + jnp.sum(up * lead[v, r, :].astype(f32), 0, keepdims=True)
        for i in range(sums.shape[0]):
            sums[i, 2 * v : 2 * v + 1, :] = first
            sums[i, 2 * v + 1 : 2 * v + 2, :] = second


def final_body(batch, own, recv, lead, sums, stats, grad_a, grad_b):
    rows = own.shape[1]
    total = sums[0]
    for i in range(1, sums.shape[0]):
        total = total + sums[i]
    total = total / batch
    for v, out in enumerate((grad_a, grad_b)):
        normal = lead[v, 0:rows, :].astype(f32)
        first, second = total[2 * v : 2 * v + 1, :], total[2 * v + 1 : 2 * v + 2, :]
        up = own[v] + recv[v]
        out[...] = ((up - first - normal * second) / stats[v : v + 1, :]).astype(bf16)


def on_device(view_a, view_b):
    rows, cols = view_a.shape
    dp_count = lax.axis_size("dp")
    feat_count = lax.axis_size("feat")
    batch = rows * dp_count
    half = batch // CORES
    part = CORES * rows // feat_count
    scale = 2.0 * off_weight / batch
    work = 2 * 2 * CORES * rows * half * cols

    views = jnp.stack([view_a, view_b])
    from_down, from_up, from_x = send(views, TO_UP), send(views, TO_DOWN), send(views, TO_X)
    sib = send(views, TO_CORE)
    far_a, far_b = send(from_down[0], TO_UP), send(from_up[1], TO_DOWN)
    x_down, x_up = send(from_x, TO_UP), send(from_x, TO_DOWN)
    x_far = send(jnp.stack([far_a, far_b]), TO_X)
    single = [far_a, far_b]
    stacked = [views, from_down, from_up, from_x, x_down, x_up, x_far]
    early = call(early_moments_body, shape(5, cols), *single, *stacked[:4])
    moments = call(
        functools.partial(late_moments_body, 5 * rows), shape(5, cols), early, *stacked[4:]
    )
    one = shape(X_HI, part, half, dtype=bf16)
    both = shape(2, *one.shape, dtype=bf16)
    four = shape(2, *both.shape, dtype=bf16)
    lead, normed, stats, *chunks = call(
        functools.partial(gram_body, batch),
        (
            shape(2, CORES * rows, cols, dtype=bf16),
            shape(2, half, cols, dtype=bf16),
            shape(3, cols),
            both,
            both,
            both,
            four,
            four,
            one,
            one,
        ),
        moments,
        send(moments, TO_CORE),
        sib,
        *single,
        *stacked,
        flops=work,
        scratch=[pltpu.VMEM((2, CORES * rows, half), bf16)],
    )
    blocks = spread_rows(reduce_rows(*chunks))
    own, other, sums = call(
        functools.partial(apply_body, scale),
        (shape(2, rows, cols), shape(2, rows, cols), shape(dp_count, 4, cols)),
        *blocks,
        normed,
        lead,
        stats,
        flops=work,
        scratch=[pltpu.VMEM((2, CORES * rows, half), bf16)],
    )
    sums = lax.all_to_all(sums, "dp", 0, 0)
    return call(
        functools.partial(final_body, batch),
        (shape(rows, cols, dtype=bf16), shape(rows, cols, dtype=bf16)),
        own,
        send(other, TO_CORE),
        lead,
        sums,
        stats,
    )


def solution(mesh):
    spec = P("dp", "feat")
    return jax.shard_map(
        on_device, mesh=mesh, in_specs=(spec, spec), out_specs=(spec, spec), check_vma=False
    )
```

```python
import functools

import jax
import jax.numpy as jnp
from jax import lax
from jax.experimental import pallas as pl
from jax.experimental.pallas import tpu as pltpu
from jax.sharding import PartitionSpec as P

off_weight = 0.0051
epsilon = 1e-05
f32 = jnp.float32
bf16 = jnp.bfloat16

X_LO, Y, CORES = 2, 4, 2


def dp_perm(move):
    def index(x, y, c):
        return (x * Y + y) * CORES + c

    return [
        (index(x, y, c), index(*move(x, y, c)))
        for x in range(X_LO)
        for y in range(Y)
        for c in range(CORES)
    ]


TO_CORE = dp_perm(lambda x, y, c: (x, y, 1 - c))
TO_X = dp_perm(lambda x, y, c: (1 - x, y, c))
TO_UP = dp_perm(lambda x, y, c: (x, (y + 1) % Y, c))
TO_DOWN = dp_perm(lambda x, y, c: (x, (y - 1) % Y, c))
TO_UP_2 = dp_perm(lambda x, y, c: (x, (y + 2) % Y, c))


X_HI, Z = 2, 8
TO_X_HI = [(q, (q + Z) % (X_HI * Z)) for q in range(X_HI * Z)]


def z_shift(step):
    return [(h * Z + z, h * Z + (z + step) % Z) for h in range(X_HI) for z in range(Z)]


def send(x, to, axis="dp"):
    return lax.ppermute(x, axis, to)


def call(body, outs, *args, flops=0, scratch=()):
    def size(s):
        return s.size * s.dtype.itemsize

    return pl.pallas_call(
        body,
        out_shape=outs,
        in_specs=[pl.BlockSpec(memory_space=pltpu.VMEM)] * len(args),
        scratch_shapes=scratch,
        out_specs=jax.tree.map(lambda _: pl.BlockSpec(memory_space=pltpu.VMEM), outs),
        compiler_params=pltpu.CompilerParams(vmem_limit_bytes=16 * 2**20),
        cost_estimate=pl.CostEstimate(
            flops=flops,
            bytes_accessed=sum(size(a) for a in args) + sum(size(o) for o in jax.tree.leaves(outs)),
            transcendentals=0,
        ),
    )(*args)


def shape(*dims, dtype=f32):
    return jax.ShapeDtypeStruct(dims, dtype)


SUB, LANE = 8, 128


def moments_body(views, out):
    rows = views.shape[1]
    a, b = views[0].astype(f32), views[1].astype(f32)
    mean_a = jnp.sum(a, 0, keepdims=True) / rows
    mean_b = jnp.sum(b, 0, keepdims=True) / rows
    a, b = a - mean_a, b - mean_b
    moments = (mean_a, mean_b, *(jnp.sum(x, 0, keepdims=True) for x in (a * a, b * b, a * b)))
    for i, value in enumerate(moments):
        for k in range(SUB):
            out[i * SUB + k : i * SUB + k + 1, :] = value[:, k * LANE : (k + 1) * LANE]


def merge(rows, *parts):
    parts = [[p[k * SUB : (k + 1) * SUB, :] for k in range(5)] for p in parts]
    mean_a, mean_b = (sum(p[k] for p in parts) / len(parts) for k in range(2))
    square_a, square_b, product = (sum(p[k] for p in parts) for k in range(2, 5))
    for p in parts:
        gap_a, gap_b = p[0] - mean_a, p[1] - mean_b
        square_a = square_a + rows * gap_a * gap_a
        square_b = square_b + rows * gap_b * gap_b
        product = product + rows * gap_a * gap_b
    return mean_a, mean_b, square_a, square_b, product


def merge_body(rows, one, other, out):
    for k, value in enumerate(merge(rows, one, other)):
        out[k * SUB : (k + 1) * SUB, :] = value


def stats_of(batch, moments, stats):
    mean_a, mean_b, square_a, square_b, product = merge(batch // len(moments), *moments)
    spread_a, spread_b = jnp.sqrt(square_a / batch + epsilon), jnp.sqrt(square_b / batch + epsilon)
    corr = product / (batch * spread_a * spread_b)
    diag = 2.0 * (corr - 1.0) - 2.0 * off_weight * corr
    for i, value in enumerate((mean_a, mean_b, spread_a, spread_b, diag)):
        for k in range(SUB):
            stats[i : i + 1, k * LANE : (k + 1) * LANE] = value[k : k + 1, :]


def normal(piece, stats, v):
    return ((piece.astype(f32) - stats[v : v + 1, :]) / stats[2 + v : 3 + v, :]).astype(bf16)


def multiply(lead, pieces, stats, normed, gram):
    rows = pieces[0][0].shape[0]
    for v in range(2):
        for i, piece in enumerate(pieces[v]):
            r = slice(i * rows, (i + 1) * rows)
            normed[v, r, :] = normal(piece[...], stats, v)
            block = lax.dot_general(
                lead[v], normed[v, r, :], (((1,), (1,)), ((), ())), preferred_element_type=f32
            )
            gram[v, :, r] = block.astype(bf16)


def split_views(pairs):
    return [[p.at[v] for p in pairs] for v in range(2)]


def stack_body(a, b, out):
    out[0] = a[...]
    out[1] = b[...]


def copy_body(x, out):
    out[...] = x[...]


def near_body(batch, *refs):
    *moments, sib, views, from_down, from_up, from_x, stats, lead, normed, gram = refs
    pairs = [views, from_down, from_up, from_x]
    rows = sib.shape[1]
    stats_of(batch, moments, stats)
    for v in range(2):
        lead[v, 0:rows, :] = normal(pairs[0][v], stats, v)
        lead[v, rows:, :] = normal(sib[v], stats, v)
    multiply(lead, split_views(pairs), stats, normed, gram)


def far_body(lead, stats, far_a, far_b, x_down, x_up, normed, gram):
    pieces = split_views([x_down, x_up])
    multiply(lead, [[far_a, *pieces[0]], [far_b, *pieces[1]]], stats, normed, gram)


def last_body(lead, stats, x_far, gram_near, gram_far, *outs):
    normed, mine, up_2, down_2, up_1, down_1, far_a, far_b, gram = outs
    rows, part = x_far.shape[1], mine.shape[2]
    near, far = gram_near.shape[2], gram_near.shape[2] + gram_far.shape[2]
    multiply(lead, split_views([x_far]), stats, normed, gram)
    z = lax.rem(lax.axis_index("feat"), Z)

    def store(ahead, v, out):
        start = lax.rem(z + ahead, Z) * part
        for h in range(X_HI):
            r = pl.ds(pl.multiple_of(start + h * rows, part), part)
            out[h, :, 0:near] = gram_near[v, r, :]
            out[h, :, near:far] = gram_far[v, r, :]
            out[h, :, far:] = gram[v, r, :]

    for v in range(2):
        store(0, v, mine.at[v])
        store(2, v, up_2.at[v])
        store(6, v, down_2.at[v])
        for i, (up, down) in enumerate(((3, 5), (1, 7))):
            store(up, v, up_1.at[i, v])
            store(down, v, down_1.at[i, v])
        store(4, v, (far_a, far_b)[v])


def fold_body(far_up, far_down, half_a, half_b, up_2, down_2, up_out, down_out):
    def plus(x, y, *z):
        total = x.astype(f32) + y.astype(f32)
        return (total + z[0].astype(f32) if z else total).astype(bf16)

    up_out[0] = plus(up_2[0], far_up[0, 0], half_a[...])
    up_out[1] = plus(up_2[1], far_up[0, 1])
    down_out[0] = plus(down_2[0], far_down[0, 0])
    down_out[1] = plus(down_2[1], far_down[0, 1], half_b[...])


def total_body(mine, near_up, near_down, far_up, far_down, out):
    total = mine[...].astype(f32) + near_up[1].astype(f32) + near_down[1].astype(f32)
    out[...] = (total + far_up[...].astype(f32) + far_down[...].astype(f32)).astype(bf16)


def add_body(a, b, out):
    out[...] = (a[...].astype(f32) + b[...].astype(f32)).astype(bf16)


def reduce_rows(mine, up_2, down_2, up_1, down_1, far_a, far_b):
    z = "feat"
    half_a = send(far_a, z_shift(2), z)
    half_b = send(far_b, z_shift(-2), z)
    from_down, from_up = send(up_1, z_shift(1), z), send(down_1, z_shift(-1), z)
    block = jax.ShapeDtypeStruct(mine.shape, bf16)
    up_2, down_2 = call(
        fold_body, (block, block), from_down, from_up, half_a, half_b, up_2, down_2
    )
    far_down, far_up = send(up_2, z_shift(2), z), send(down_2, z_shift(-2), z)
    total = call(total_body, block, mine, from_down, from_up, far_down, far_up)
    return call(add_body, block, total, send(total, TO_X_HI, z))


def spread_rows(block):
    z = "feat"
    from_1 = send(block, z_shift(1), z)
    from_7 = send(block, z_shift(-1), z)
    from_2 = send(block, z_shift(2), z)
    from_6 = send(block, z_shift(-2), z)
    from_3 = send(from_2, z_shift(1), z)
    from_5 = send(from_6, z_shift(-1), z)
    from_4a = send(from_2[0], z_shift(2), z)
    from_4b = send(from_6[1], z_shift(-2), z)
    return [block, from_1, from_2, from_3, from_5, from_6, from_7, from_4a, from_4b]


def apply_body(scale, *refs):
    *blocks, from_4a, from_4b, near, far, last, lead, stats, own, other, sums, gram = refs
    rows, part = own.shape[1], blocks[0].shape[2]
    z = lax.rem(lax.axis_index("feat"), Z)

    def load(back, v, block):
        start = lax.rem(z + Z - back, Z) * part
        for h in range(X_HI):
            gram[v, pl.ds(pl.multiple_of(start + h * rows, part), part), :] = block[h]

    for v in range(2):
        for back, block in zip((0, 1, 2, 3, 5, 6, 7), blocks):
            load(back, v, block.at[v])
        load(4, v, (from_4a, from_4b)[v])
    diag = stats[4:5, :]
    ends = (0, near.shape[1], near.shape[1] + far.shape[1], gram.shape[2])
    for v in range(2):
        first = second = 0.0
        for h, out in enumerate((own, other)):
            r = slice(h * rows, (h + 1) * rows)
            up = 0.0
            for i, normed in enumerate((near, far, last)):
                left = gram[1 - v, r, ends[i] : ends[i + 1]]
                up = up + jnp.dot(left, normed[v], preferred_element_type=f32)
            up = scale * up
            if h == 0:
                up = up + lead[1 - v, r, :].astype(f32) * diag
            out[v] = up
            first = first + jnp.sum(up, 0, keepdims=True)
            second = second + jnp.sum(up * lead[v, r, :].astype(f32), 0, keepdims=True)
        for i in range(sums.shape[0]):
            sums[i, 2 * v : 2 * v + 1, :] = first
            sums[i, 2 * v + 1 : 2 * v + 2, :] = second


def final_body(batch, own, recv, lead, sums, stats, grad_a, grad_b):
    rows = own.shape[1]
    total = sums[0]
    for i in range(1, sums.shape[0]):
        total = total + sums[i]
    total = total / batch
    for v, out in enumerate((grad_a, grad_b)):
        own_normed = lead[v, 0:rows, :].astype(f32)
        first, second = total[2 * v : 2 * v + 1, :], total[2 * v + 1 : 2 * v + 2, :]
        up = own[v] + recv[v]
        out[...] = ((up - first - own_normed * second) / stats[2 + v : 3 + v, :]).astype(bf16)


def on_device(view_a, view_b):
    rows, cols = view_a.shape
    dp_count = lax.axis_size("dp")
    feat_count = lax.axis_size("feat")
    batch = rows * dp_count
    half = batch // CORES
    part = CORES * rows // feat_count
    scale = 2.0 * off_weight / batch
    work = 2 * 2 * CORES * rows * half * cols

    views = jnp.stack([view_a, view_b])
    from_down, from_up = send(views, TO_UP), send(views, TO_DOWN)
    sib = send(views, TO_CORE)
    moments = call(moments_body, shape(5 * SUB, LANE), views)
    for rank, to in enumerate((TO_CORE, TO_X)):
        body = functools.partial(merge_body, rows * 2**rank)
        moments = call(body, shape(5 * SUB, LANE), moments, send(moments, to))
    late_views, moments = lax.optimization_barrier((views, moments))
    from_x = send(late_views, TO_X)
    moments = [moments, *(send(moments, to) for to in (TO_UP, TO_DOWN, TO_UP_2))]
    from_down, from_up, moments[2] = lax.optimization_barrier((from_down, from_up, moments[2]))
    from_x, moments[3] = lax.optimization_barrier((from_x, moments[3]))
    far_a, far_b = send(from_down[0], TO_UP), send(from_up[1], TO_DOWN)
    from_x = call(copy_body, jax.ShapeDtypeStruct(from_x.shape, bf16), from_x, flops=10**10)
    x_down, x_up = send(from_x, TO_UP), send(from_x, TO_DOWN)
    far = call(stack_body, jax.ShapeDtypeStruct(views.shape, bf16), far_a, far_b, flops=10**10)
    x_far = send(far, TO_X)

    def results(pieces):
        return (
            shape(2, pieces * rows, cols, dtype=bf16),
            shape(2, CORES * rows, pieces * rows, dtype=bf16),
        )

    stats, lead, near, gram_near = call(
        functools.partial(near_body, batch),
        (shape(5, cols), shape(2, CORES * rows, cols, dtype=bf16), *results(4)),
        *moments,
        sib,
        views,
        from_down,
        from_up,
        from_x,
        flops=work // 2,
    )
    far, gram_far = call(
        far_body, results(3), lead, stats, far_a, far_b, x_down, x_up, flops=work * 3 // 8
    )
    one = shape(X_HI, part, half, dtype=bf16)
    both = shape(2, *one.shape, dtype=bf16)
    four = shape(2, *both.shape, dtype=bf16)
    last, *chunks = call(
        last_body,
        (results(1)[0], both, both, both, four, four, one, one),
        lead,
        stats,
        x_far,
        gram_near,
        gram_far,
        flops=work // 8,
        scratch=[pltpu.VMEM(results(1)[1].shape, bf16)],
    )
    blocks = spread_rows(reduce_rows(*chunks))
    own, other, sums = call(
        functools.partial(apply_body, scale),
        (shape(2, rows, cols), shape(2, rows, cols), shape(dp_count, 4, cols)),
        *blocks,
        near,
        far,
        last,
        lead,
        stats,
        flops=work,
        scratch=[pltpu.VMEM((2, CORES * rows, half), bf16)],
    )
    sums = lax.all_to_all(sums, "dp", 0, 0)
    return call(
        functools.partial(final_body, batch),
        (shape(rows, cols, dtype=bf16), shape(rows, cols, dtype=bf16)),
        own,
        send(other, TO_CORE),
        lead,
        sums,
        stats,
    )


def solution(mesh):
    spec = P("dp", "feat")
    return jax.shard_map(
        on_device, mesh=mesh, in_specs=(spec, spec), out_specs=(spec, spec), check_vma=False
    )
```

```python
import functools

import jax
import jax.numpy as jnp
from jax import lax
from jax.experimental import pallas as pl
from jax.experimental.pallas import tpu as pltpu
from jax.sharding import PartitionSpec as P

off_weight = 0.0051
epsilon = 1e-05
f32 = jnp.float32
bf16 = jnp.bfloat16

X_LO, Y, CORES = 2, 4, 2


def dp_perm(move):
    def index(x, y, c):
        return (x * Y + y) * CORES + c

    return [
        (index(x, y, c), index(*move(x, y, c)))
        for x in range(X_LO)
        for y in range(Y)
        for c in range(CORES)
    ]


TO_CORE = dp_perm(lambda x, y, c: (x, y, 1 - c))
TO_X = dp_perm(lambda x, y, c: (1 - x, y, c))
TO_UP = dp_perm(lambda x, y, c: (x, (y + 1) % Y, c))
TO_DOWN = dp_perm(lambda x, y, c: (x, (y - 1) % Y, c))


X_HI, Z = 2, 8
TO_X_HI = [(q, (q + Z) % (X_HI * Z)) for q in range(X_HI * Z)]


def z_shift(step):
    return [(h * Z + z, h * Z + (z + step) % Z) for h in range(X_HI) for z in range(Z)]


def send(x, to, axis="dp"):
    return lax.ppermute(x, axis, to)


def call(body, outs, *args, flops=0, scratch=()):
    def size(s):
        return s.size * s.dtype.itemsize

    return pl.pallas_call(
        body,
        out_shape=outs,
        in_specs=[pl.BlockSpec(memory_space=pltpu.VMEM)] * len(args),
        scratch_shapes=scratch,
        out_specs=jax.tree.map(lambda _: pl.BlockSpec(memory_space=pltpu.VMEM), outs),
        compiler_params=pltpu.CompilerParams(vmem_limit_bytes=16 * 2**20),
        cost_estimate=pl.CostEstimate(
            flops=flops,
            bytes_accessed=sum(size(a) for a in args) + sum(size(o) for o in jax.tree.leaves(outs)),
            transcendentals=0,
        ),
    )(*args)


def shape(*dims, dtype=f32):
    return jax.ShapeDtypeStruct(dims, dtype)


SUB, LANE = 8, 128


def moments_body(views, out):
    rows = views.shape[1]
    a, b = views[0].astype(f32), views[1].astype(f32)
    mean_a = jnp.sum(a, 0, keepdims=True) / rows
    mean_b = jnp.sum(b, 0, keepdims=True) / rows
    a, b = a - mean_a, b - mean_b
    moments = (mean_a, mean_b, *(jnp.sum(x, 0, keepdims=True) for x in (a * a, b * b, a * b)))
    for i, value in enumerate(moments):
        for k in range(SUB):
            out[i * SUB + k : i * SUB + k + 1, :] = value[:, k * LANE : (k + 1) * LANE]


def merge(rows, *parts):
    parts = [[p[k * SUB : (k + 1) * SUB, :] for k in range(5)] for p in parts]
    mean_a, mean_b = (sum(p[k] for p in parts) / len(parts) for k in range(2))
    square_a, square_b, product = (sum(p[k] for p in parts) for k in range(2, 5))
    for p in parts:
        gap_a, gap_b = p[0] - mean_a, p[1] - mean_b
        square_a = square_a + rows * gap_a * gap_a
        square_b = square_b + rows * gap_b * gap_b
        product = product + rows * gap_a * gap_b
    return mean_a, mean_b, square_a, square_b, product


def merge_body(rows, *refs):
    *parts, out = refs
    for k, value in enumerate(merge(rows, *parts)):
        out[k * SUB : (k + 1) * SUB, :] = value


def stats_of(batch, moments, stats):
    mean_a, mean_b, square_a, square_b, product = merge(batch // len(moments), *moments)
    spread_a, spread_b = jnp.sqrt(square_a / batch + epsilon), jnp.sqrt(square_b / batch + epsilon)
    corr = product / (batch * spread_a * spread_b)
    diag = 2.0 * (corr - 1.0) - 2.0 * off_weight * corr
    for i, value in enumerate((mean_a, mean_b, spread_a, spread_b, diag)):
        for k in range(SUB):
            stats[i : i + 1, k * LANE : (k + 1) * LANE] = value[k : k + 1, :]


def normal(piece, stats, v):
    return ((piece.astype(f32) - stats[v : v + 1, :]) / stats[2 + v : 3 + v, :]).astype(bf16)


def multiply(lead, pieces, stats, normed, gram):
    rows = pieces[0][0].shape[0]
    for v in range(2):
        for i, piece in enumerate(pieces[v]):
            r = slice(i * rows, (i + 1) * rows)
            normed[v, r, :] = normal(piece[...], stats, v)
            block = lax.dot_general(
                lead[v], normed[v, r, :], (((1,), (1,)), ((), ())), preferred_element_type=f32
            )
            gram[v, :, r] = block.astype(bf16)


def split_views(pairs):
    return [[p.at[v] for p in pairs] for v in range(2)]


def stack_body(a, b, out):
    out[0] = a[...]
    out[1] = b[...]


def copy_body(x, out):
    out[...] = x[...]


def near_body(batch, *refs):
    *moments, sib, views, from_down, from_up, from_x, stats, lead, normed, gram = refs
    pairs = [views, from_down, from_up, from_x]
    rows = sib.shape[1]
    stats_of(batch, moments, stats)
    for v in range(2):
        lead[v, 0:rows, :] = normal(pairs[0][v], stats, v)
        lead[v, rows:, :] = normal(sib[v], stats, v)
    multiply(lead, split_views(pairs), stats, normed, gram)


def far_body(lead, stats, far_a, far_b, x_down, x_up, normed, gram):
    pieces = split_views([x_down, x_up])
    multiply(lead, [[far_a, *pieces[0]], [far_b, *pieces[1]]], stats, normed, gram)


def last_body(lead, stats, x_far, gram_near, gram_far, *outs):
    normed, mine, up_2, down_2, up_1, down_1, far_a, far_b, gram = outs
    rows, part = x_far.shape[1], mine.shape[2]
    near, far = gram_near.shape[2], gram_near.shape[2] + gram_far.shape[2]
    multiply(lead, split_views([x_far]), stats, normed, gram)
    z = lax.rem(lax.axis_index("feat"), Z)

    def store(ahead, v, out):
        start = lax.rem(z + ahead, Z) * part
        for h in range(X_HI):
            r = pl.ds(pl.multiple_of(start + h * rows, part), part)
            out[h, :, 0:near] = gram_near[v, r, :]
            out[h, :, near:far] = gram_far[v, r, :]
            out[h, :, far:] = gram[v, r, :]

    for v in range(2):
        store(0, v, mine.at[v])
        store(2, v, up_2.at[v])
        store(6, v, down_2.at[v])
        for i, (up, down) in enumerate(((3, 5), (1, 7))):
            store(up, v, up_1.at[i, v])
            store(down, v, down_1.at[i, v])
        store(4, v, (far_a, far_b)[v])


def fold_body(far_up, far_down, half_a, half_b, up_2, down_2, up_out, down_out):
    def plus(x, y, *z):
        total = x.astype(f32) + y.astype(f32)
        return (total + z[0].astype(f32) if z else total).astype(bf16)

    up_out[0] = plus(up_2[0], far_up[0, 0], half_a[...])
    up_out[1] = plus(up_2[1], far_up[0, 1])
    down_out[0] = plus(down_2[0], far_down[0, 0])
    down_out[1] = plus(down_2[1], far_down[0, 1], half_b[...])


def total_body(mine, near_up, near_down, far_up, far_down, out):
    total = mine[...].astype(f32) + near_up[1].astype(f32) + near_down[1].astype(f32)
    out[...] = (total + far_up[...].astype(f32) + far_down[...].astype(f32)).astype(bf16)


def add_body(a, b, out):
    out[...] = (a[...].astype(f32) + b[...].astype(f32)).astype(bf16)


def reduce_rows(mine, up_2, down_2, up_1, down_1, far_a, far_b):
    z = "feat"
    half_a = send(far_a, z_shift(2), z)
    half_b = send(far_b, z_shift(-2), z)
    from_down, from_up = send(up_1, z_shift(1), z), send(down_1, z_shift(-1), z)
    block = jax.ShapeDtypeStruct(mine.shape, bf16)
    up_2, down_2 = call(
        fold_body, (block, block), from_down, from_up, half_a, half_b, up_2, down_2
    )
    far_down, far_up = send(up_2, z_shift(2), z), send(down_2, z_shift(-2), z)
    total = call(total_body, block, mine, from_down, from_up, far_down, far_up)
    return call(add_body, block, total, send(total, TO_X_HI, z))


def spread_rows(block):
    z = "feat"
    from_1 = send(block, z_shift(1), z)
    from_7 = send(block, z_shift(-1), z)
    from_2 = send(block, z_shift(2), z)
    from_6 = send(block, z_shift(-2), z)
    from_3 = send(from_2, z_shift(1), z)
    from_5 = send(from_6, z_shift(-1), z)
    from_4a = send(from_2[0], z_shift(2), z)
    from_4b = send(from_6[1], z_shift(-2), z)
    return [block, from_1, from_2, from_3, from_5, from_6, from_7, from_4a, from_4b]


def apply_body(scale, *refs):
    *blocks, from_4a, from_4b, near, far, last, lead, stats, own, other, sums, gram = refs
    rows, part = own.shape[1], blocks[0].shape[2]
    z = lax.rem(lax.axis_index("feat"), Z)

    def load(back, v, block):
        start = lax.rem(z + Z - back, Z) * part
        for h in range(X_HI):
            gram[v, pl.ds(pl.multiple_of(start + h * rows, part), part), :] = block[h]

    for v in range(2):
        for back, block in zip((0, 1, 2, 3, 5, 6, 7), blocks):
            load(back, v, block.at[v])
        load(4, v, (from_4a, from_4b)[v])
    diag = stats[4:5, :]
    ends = (0, near.shape[1], near.shape[1] + far.shape[1], gram.shape[2])
    for v in range(2):
        first = second = 0.0
        for h, out in enumerate((own, other)):
            r = slice(h * rows, (h + 1) * rows)
            up = 0.0
            for i, normed in enumerate((near, far, last)):
                left = gram[1 - v, r, ends[i] : ends[i + 1]]
                up = up + jnp.dot(left, normed[v], preferred_element_type=f32)
            up = scale * up
            if h == 0:
                up = up + lead[1 - v, r, :].astype(f32) * diag
            out[v] = up
            first = first + jnp.sum(up, 0, keepdims=True)
            second = second + jnp.sum(up * lead[v, r, :].astype(f32), 0, keepdims=True)
        for i in range(sums.shape[0]):
            sums[i, 2 * v : 2 * v + 1, :] = first
            sums[i, 2 * v + 1 : 2 * v + 2, :] = second


def final_body(batch, own, recv, lead, sums, stats, grad_a, grad_b):
    rows = own.shape[1]
    total = sums[0]
    for i in range(1, sums.shape[0]):
        total = total + sums[i]
    total = total / batch
    for v, out in enumerate((grad_a, grad_b)):
        own_normed = lead[v, 0:rows, :].astype(f32)
        first, second = total[2 * v : 2 * v + 1, :], total[2 * v + 1 : 2 * v + 2, :]
        up = own[v] + recv[v]
        out[...] = ((up - first - own_normed * second) / stats[2 + v : 3 + v, :]).astype(bf16)


def on_device(view_a, view_b):
    rows, cols = view_a.shape
    dp_count = lax.axis_size("dp")
    feat_count = lax.axis_size("feat")
    batch = rows * dp_count
    half = batch // CORES
    part = CORES * rows // feat_count
    scale = 2.0 * off_weight / batch
    work = 2 * 2 * CORES * rows * half * cols

    views = jnp.stack([view_a, view_b])
    from_down, from_up, from_x = send(views, TO_UP), send(views, TO_DOWN), send(views, TO_X)
    sib = send(views, TO_CORE)
    tile = shape(5 * SUB, LANE)
    moments = call(moments_body, tile, views)
    moments = call(
        functools.partial(merge_body, rows), tile, moments, send(moments, TO_CORE)
    )
    below, above = send(moments, TO_UP), send(moments, TO_DOWN)
    from_down, from_up, below, above = lax.optimization_barrier((from_down, from_up, below, above))
    opposite = send(below, TO_UP)
    from_x, opposite = lax.optimization_barrier((from_x, opposite))
    moments = call(
        functools.partial(merge_body, CORES * rows), tile, moments, below, above, opposite
    )
    moments_x = send(moments, TO_X)
    far_a, far_b = send(from_down[0], TO_UP), send(from_up[1], TO_DOWN)
    from_x = call(copy_body, jax.ShapeDtypeStruct(from_x.shape, bf16), from_x, flops=10**10)
    x_down, x_up = send(from_x, TO_UP), send(from_x, TO_DOWN)
    far_b, moments_x = lax.optimization_barrier((far_b, moments_x))
    far = call(stack_body, jax.ShapeDtypeStruct(views.shape, bf16), far_a, far_b, flops=10**10)
    x_far = send(far, TO_X)

    def results(pieces):
        return (
            shape(2, pieces * rows, cols, dtype=bf16),
            shape(2, CORES * rows, pieces * rows, dtype=bf16),
        )

    stats, lead, near, gram_near = call(
        functools.partial(near_body, batch),
        (shape(5, cols), shape(2, CORES * rows, cols, dtype=bf16), *results(4)),
        moments,
        moments_x,
        sib,
        views,
        from_down,
        from_up,
        from_x,
        flops=work // 2,
    )
    far, gram_far = call(
        far_body, results(3), lead, stats, far_a, far_b, x_down, x_up, flops=work * 3 // 8
    )
    one = shape(X_HI, part, half, dtype=bf16)
    both = shape(2, *one.shape, dtype=bf16)
    four = shape(2, *both.shape, dtype=bf16)
    last, *chunks = call(
        last_body,
        (results(1)[0], both, both, both, four, four, one, one),
        lead,
        stats,
        x_far,
        gram_near,
        gram_far,
        flops=work // 8,
        scratch=[pltpu.VMEM(results(1)[1].shape, bf16)],
    )
    blocks = spread_rows(reduce_rows(*chunks))
    own, other, sums = call(
        functools.partial(apply_body, scale),
        (shape(2, rows, cols), shape(2, rows, cols), shape(dp_count, 4, cols)),
        *blocks,
        near,
        far,
        last,
        lead,
        stats,
        flops=work,
        scratch=[pltpu.VMEM((2, CORES * rows, half), bf16)],
    )
    sums = lax.all_to_all(sums, "dp", 0, 0)
    return call(
        functools.partial(final_body, batch),
        (shape(rows, cols, dtype=bf16), shape(rows, cols, dtype=bf16)),
        own,
        send(other, TO_CORE),
        lead,
        sums,
        stats,
    )


def solution(mesh):
    spec = P("dp", "feat")
    return jax.shard_map(
        on_device, mesh=mesh, in_specs=(spec, spec), out_specs=(spec, spec), check_vma=False
    )
```

```python
import functools

import jax
import jax.numpy as jnp
from jax import lax
from jax.experimental import pallas as pl
from jax.experimental.pallas import tpu as pltpu
from jax.sharding import PartitionSpec as P

off_weight = 0.0051
epsilon = 1e-05
f32 = jnp.float32
bf16 = jnp.bfloat16

X_LO, Y, CORES = 2, 4, 2


def dp_perm(move):
    def index(x, y, c):
        return (x * Y + y) * CORES + c

    return [
        (index(x, y, c), index(*move(x, y, c)))
        for x in range(X_LO)
        for y in range(Y)
        for c in range(CORES)
    ]


TO_CORE = dp_perm(lambda x, y, c: (x, y, 1 - c))
TO_X = dp_perm(lambda x, y, c: (1 - x, y, c))
TO_UP = dp_perm(lambda x, y, c: (x, (y + 1) % Y, c))
TO_DOWN = dp_perm(lambda x, y, c: (x, (y - 1) % Y, c))


X_HI, Z = 2, 8
TO_X_HI = [(q, (q + Z) % (X_HI * Z)) for q in range(X_HI * Z)]


def z_shift(step):
    return [(h * Z + z, h * Z + (z + step) % Z) for h in range(X_HI) for z in range(Z)]


def send(x, to, axis="dp"):
    return lax.ppermute(x, axis, to)


def call(body, outs, *args, flops=0, scratch=()):
    def size(s):
        return s.size * s.dtype.itemsize

    return pl.pallas_call(
        body,
        out_shape=outs,
        in_specs=[pl.BlockSpec(memory_space=pltpu.VMEM)] * len(args),
        scratch_shapes=scratch,
        out_specs=jax.tree.map(lambda _: pl.BlockSpec(memory_space=pltpu.VMEM), outs),
        compiler_params=pltpu.CompilerParams(vmem_limit_bytes=16 * 2**20),
        cost_estimate=pl.CostEstimate(
            flops=flops,
            bytes_accessed=sum(size(a) for a in args) + sum(size(o) for o in jax.tree.leaves(outs)),
            transcendentals=0,
        ),
    )(*args)


def shape(*dims, dtype=f32):
    return jax.ShapeDtypeStruct(dims, dtype)


SUB, LANE = 8, 128


def moments_body(views, out):
    rows = views.shape[1]
    a, b = views[0].astype(f32), views[1].astype(f32)
    mean_a = jnp.sum(a, 0, keepdims=True) / rows
    mean_b = jnp.sum(b, 0, keepdims=True) / rows
    a, b = a - mean_a, b - mean_b
    moments = (mean_a, mean_b, *(jnp.sum(x, 0, keepdims=True) for x in (a * a, b * b, a * b)))
    for i, value in enumerate(moments):
        for k in range(SUB):
            out[i * SUB + k : i * SUB + k + 1, :] = value[:, k * LANE : (k + 1) * LANE]


def merge(rows, *parts):
    parts = [[p[k * SUB : (k + 1) * SUB, :] for k in range(5)] for p in parts]
    mean_a, mean_b = (sum(p[k] for p in parts) / len(parts) for k in range(2))
    square_a, square_b, product = (sum(p[k] for p in parts) for k in range(2, 5))
    for p in parts:
        gap_a, gap_b = p[0] - mean_a, p[1] - mean_b
        square_a = square_a + rows * gap_a * gap_a
        square_b = square_b + rows * gap_b * gap_b
        product = product + rows * gap_a * gap_b
    return mean_a, mean_b, square_a, square_b, product


def merge_body(rows, *refs):
    *parts, out = refs
    for k, value in enumerate(merge(rows, *parts)):
        out[k * SUB : (k + 1) * SUB, :] = value


def stats_of(batch, moments, stats):
    mean_a, mean_b, square_a, square_b, product = merge(batch // len(moments), *moments)
    spread_a, spread_b = jnp.sqrt(square_a / batch + epsilon), jnp.sqrt(square_b / batch + epsilon)
    corr = product / (batch * spread_a * spread_b)
    diag = 2.0 * (corr - 1.0) - 2.0 * off_weight * corr
    for i, value in enumerate((mean_a, mean_b, spread_a, spread_b, diag)):
        for k in range(SUB):
            stats[i : i + 1, k * LANE : (k + 1) * LANE] = value[k : k + 1, :]


def normal(piece, stats, v):
    return ((piece.astype(f32) - stats[v : v + 1, :]) / stats[2 + v : 3 + v, :]).astype(bf16)


def multiply(lead, pieces, stats, normed, gram):
    rows = pieces[0][0].shape[0]
    for v in range(2):
        for i, piece in enumerate(pieces[v]):
            r = slice(i * rows, (i + 1) * rows)
            normed[v, r, :] = normal(piece[...], stats, v)
            block = lax.dot_general(
                lead[v], normed[v, r, :], (((1,), (1,)), ((), ())), preferred_element_type=f32
            )
            gram[v, :, r] = block.astype(bf16)


def split_views(pairs):
    return [[p.at[v] for p in pairs] for v in range(2)]


def stack_body(a, b, out):
    out[0] = a[...]
    out[1] = b[...]


def copy_body(x, out):
    out[...] = x[...]


def near_body(batch, *refs):
    *moments, sib, views, from_down, from_up, from_x, stats, lead, normed, gram = refs
    pairs = [views, from_down, from_up, from_x]
    rows = sib.shape[1]
    stats_of(batch, moments, stats)
    for v in range(2):
        lead[v, 0:rows, :] = normal(pairs[0][v], stats, v)
        lead[v, rows:, :] = normal(sib[v], stats, v)
    multiply(lead, split_views(pairs), stats, normed, gram)


def last_body(lead, stats, opp_a, opp_b, x_down, x_up, x_far, gram_near, *outs):
    normed, mine, up_2, down_2, up_1, down_1, far_a, far_b, gram = outs
    rows, part = x_far.shape[1], mine.shape[2]
    middle = gram_near.shape[2]
    pieces = split_views([x_down, x_up, x_far])
    multiply(lead, [[opp_a, *pieces[0]], [opp_b, *pieces[1]]], stats, normed, gram)
    z = lax.rem(lax.axis_index("feat"), Z)

    def store(ahead, v, out):
        start = lax.rem(z + ahead, Z) * part
        for h in range(X_HI):
            r = pl.ds(pl.multiple_of(start + h * rows, part), part)
            out[h, :, 0:middle] = gram_near[v, r, :]
            out[h, :, middle:] = gram[v, r, :]

    for v in range(2):
        store(0, v, mine.at[v])
        store(2, v, up_2.at[v])
        store(6, v, down_2.at[v])
        for i, (up, down) in enumerate(((3, 5), (1, 7))):
            store(up, v, up_1.at[i, v])
            store(down, v, down_1.at[i, v])
        store(4, v, (far_a, far_b)[v])


def fold_body(far_up, far_down, half_a, half_b, up_2, down_2, up_out, down_out):
    def plus(x, y, *z):
        total = x.astype(f32) + y.astype(f32)
        return (total + z[0].astype(f32) if z else total).astype(bf16)

    up_out[0] = plus(up_2[0], far_up[0, 0], half_a[...])
    up_out[1] = plus(up_2[1], far_up[0, 1])
    down_out[0] = plus(down_2[0], far_down[0, 0])
    down_out[1] = plus(down_2[1], far_down[0, 1], half_b[...])


def total_body(mine, near_up, near_down, far_up, far_down, out):
    total = mine[...].astype(f32) + near_up[1].astype(f32) + near_down[1].astype(f32)
    out[...] = (total + far_up[...].astype(f32) + far_down[...].astype(f32)).astype(bf16)


def add_body(a, b, out):
    out[...] = (a[...].astype(f32) + b[...].astype(f32)).astype(bf16)


def reduce_rows(mine, up_2, down_2, up_1, down_1, far_a, far_b):
    z = "feat"
    half_a = send(far_a, z_shift(2), z)
    half_b = send(far_b, z_shift(-2), z)
    from_down, from_up = send(up_1, z_shift(1), z), send(down_1, z_shift(-1), z)
    block = jax.ShapeDtypeStruct(mine.shape, bf16)
    up_2, down_2 = call(
        fold_body, (block, block), from_down, from_up, half_a, half_b, up_2, down_2
    )
    far_down, far_up = send(up_2, z_shift(2), z), send(down_2, z_shift(-2), z)
    total = call(total_body, block, mine, from_down, from_up, far_down, far_up)
    return call(add_body, block, total, send(total, TO_X_HI, z))


def spread_rows(block):
    z = "feat"
    from_1 = send(block, z_shift(1), z)
    from_7 = send(block, z_shift(-1), z)
    from_2 = send(block, z_shift(2), z)
    from_6 = send(block, z_shift(-2), z)
    from_3 = send(from_2, z_shift(1), z)
    from_5 = send(from_6, z_shift(-1), z)
    from_4a = send(from_2[0], z_shift(2), z)
    from_4b = send(from_6[1], z_shift(-2), z)
    return [block, from_1, from_2, from_3, from_5, from_6, from_7, from_4a, from_4b]


def apply_body(scale, *refs):
    *blocks, from_4a, from_4b, near, last, lead, stats, own, other, sums, gram = refs
    rows, part = own.shape[1], blocks[0].shape[2]
    z = lax.rem(lax.axis_index("feat"), Z)

    def load(back, v, block):
        start = lax.rem(z + Z - back, Z) * part
        for h in range(X_HI):
            gram[v, pl.ds(pl.multiple_of(start + h * rows, part), part), :] = block[h]

    for v in range(2):
        for back, block in zip((0, 1, 2, 3, 5, 6, 7), blocks):
            load(back, v, block.at[v])
        load(4, v, (from_4a, from_4b)[v])
    diag = stats[4:5, :]
    ends = (0, near.shape[1], gram.shape[2])
    for v in range(2):
        first = second = 0.0
        for h, out in enumerate((own, other)):
            r = slice(h * rows, (h + 1) * rows)
            up = 0.0
            for i, normed in enumerate((near, last)):
                left = gram[1 - v, r, ends[i] : ends[i + 1]]
                up = up + jnp.dot(left, normed[v], preferred_element_type=f32)
            up = scale * up
            if h == 0:
                up = up + lead[1 - v, r, :].astype(f32) * diag
            out[v] = up
            first = first + jnp.sum(up, 0, keepdims=True)
            second = second + jnp.sum(up * lead[v, r, :].astype(f32), 0, keepdims=True)
        for i in range(sums.shape[0]):
            sums[i, 2 * v : 2 * v + 1, :] = first
            sums[i, 2 * v + 1 : 2 * v + 2, :] = second


def final_body(batch, own, recv, lead, sums, stats, grad_a, grad_b):
    rows = own.shape[1]
    total = sums[0]
    for i in range(1, sums.shape[0]):
        total = total + sums[i]
    total = total / batch
    for v, out in enumerate((grad_a, grad_b)):
        own_normed = lead[v, 0:rows, :].astype(f32)
        first, second = total[2 * v : 2 * v + 1, :], total[2 * v + 1 : 2 * v + 2, :]
        up = own[v] + recv[v]
        out[...] = ((up - first - own_normed * second) / stats[2 + v : 3 + v, :]).astype(bf16)


def on_device(view_a, view_b):
    rows, cols = view_a.shape
    dp_count = lax.axis_size("dp")
    feat_count = lax.axis_size("feat")
    batch = rows * dp_count
    half = batch // CORES
    part = CORES * rows // feat_count
    scale = 2.0 * off_weight / batch
    work = 2 * 2 * CORES * rows * half * cols

    views = jnp.stack([view_a, view_b])
    from_down, from_up, from_x = send(views, TO_UP), send(views, TO_DOWN), send(views, TO_X)
    sib = send(views, TO_CORE)
    tile = shape(5 * SUB, LANE)
    moments = call(moments_body, tile, views)
    moments = call(
        functools.partial(merge_body, rows), tile, moments, send(moments, TO_CORE)
    )
    below, above = send(moments, TO_UP), send(moments, TO_DOWN)
    from_down, from_up, below, above = lax.optimization_barrier((from_down, from_up, below, above))
    opposite = send(below, TO_UP)
    from_x, opposite = lax.optimization_barrier((from_x, opposite))
    moments = call(
        functools.partial(merge_body, CORES * rows), tile, moments, below, above, opposite
    )
    moments_x = send(moments, TO_X)
    far_a, far_b = send(from_down[0], TO_UP), send(from_up[1], TO_DOWN)
    from_x = call(copy_body, jax.ShapeDtypeStruct(from_x.shape, bf16), from_x, flops=10**10)
    x_down, x_up = send(from_x, TO_UP), send(from_x, TO_DOWN)
    far_b, moments_x = lax.optimization_barrier((far_b, moments_x))
    far = call(stack_body, jax.ShapeDtypeStruct(views.shape, bf16), far_a, far_b, flops=10**10)
    x_far = send(far, TO_X)

    def results(pieces):
        return (
            shape(2, pieces * rows, cols, dtype=bf16),
            shape(2, CORES * rows, pieces * rows, dtype=bf16),
        )

    stats, lead, near, gram_near = call(
        functools.partial(near_body, batch),
        (shape(5, cols), shape(2, CORES * rows, cols, dtype=bf16), *results(4)),
        moments,
        moments_x,
        sib,
        views,
        from_down,
        from_up,
        from_x,
        flops=work // 2,
    )
    one = shape(X_HI, part, half, dtype=bf16)
    both = shape(2, *one.shape, dtype=bf16)
    four = shape(2, *both.shape, dtype=bf16)
    last, *chunks = call(
        last_body,
        (results(4)[0], both, both, both, four, four, one, one),
        lead,
        stats,
        far_a,
        far_b,
        x_down,
        x_up,
        x_far,
        gram_near,
        flops=work // 2,
        scratch=[pltpu.VMEM(results(4)[1].shape, bf16)],
    )
    blocks = spread_rows(reduce_rows(*chunks))
    own, other, sums = call(
        functools.partial(apply_body, scale),
        (shape(2, rows, cols), shape(2, rows, cols), shape(dp_count, 4, cols)),
        *blocks,
        near,
        last,
        lead,
        stats,
        flops=work,
        scratch=[pltpu.VMEM((2, CORES * rows, half), bf16)],
    )
    sums = lax.all_to_all(sums, "dp", 0, 0)
    return call(
        functools.partial(final_body, batch),
        (shape(rows, cols, dtype=bf16), shape(rows, cols, dtype=bf16)),
        own,
        send(other, TO_CORE),
        lead,
        sums,
        stats,
    )


def solution(mesh):
    spec = P("dp", "feat")
    return jax.shard_map(
        on_device, mesh=mesh, in_specs=(spec, spec), out_specs=(spec, spec), check_vma=False
    )
```

```python
import functools

import jax
import jax.numpy as jnp
from jax import lax
from jax.experimental import pallas as pl
from jax.experimental.pallas import tpu as pltpu
from jax.sharding import PartitionSpec as P

off_weight = 0.0051
epsilon = 1e-05
f32 = jnp.float32
bf16 = jnp.bfloat16

X_LO, Y, CORES = 2, 4, 2


def dp_perm(move):
    def index(x, y, c):
        return (x * Y + y) * CORES + c

    return [
        (index(x, y, c), index(*move(x, y, c)))
        for x in range(X_LO)
        for y in range(Y)
        for c in range(CORES)
    ]


TO_CORE = dp_perm(lambda x, y, c: (x, y, 1 - c))
TO_X = dp_perm(lambda x, y, c: (1 - x, y, c))
TO_UP = dp_perm(lambda x, y, c: (x, (y + 1) % Y, c))
TO_DOWN = dp_perm(lambda x, y, c: (x, (y - 1) % Y, c))


X_HI, Z = 2, 8
TO_X_HI = [(q, (q + Z) % (X_HI * Z)) for q in range(X_HI * Z)]


def z_shift(step):
    return [(h * Z + z, h * Z + (z + step) % Z) for h in range(X_HI) for z in range(Z)]


def send(x, to, axis="dp"):
    return lax.ppermute(x, axis, to)


def call(body, outs, *args, flops=0, scratch=()):
    def size(s):
        return s.size * s.dtype.itemsize

    return pl.pallas_call(
        body,
        out_shape=outs,
        in_specs=[pl.BlockSpec(memory_space=pltpu.VMEM)] * len(args),
        scratch_shapes=scratch,
        out_specs=jax.tree.map(lambda _: pl.BlockSpec(memory_space=pltpu.VMEM), outs),
        compiler_params=pltpu.CompilerParams(vmem_limit_bytes=16 * 2**20),
        cost_estimate=pl.CostEstimate(
            flops=flops,
            bytes_accessed=sum(size(a) for a in args) + sum(size(o) for o in jax.tree.leaves(outs)),
            transcendentals=0,
        ),
    )(*args)


def shape(*dims, dtype=f32):
    return jax.ShapeDtypeStruct(dims, dtype)


SUB, LANE = 8, 128


def moments_body(views, out):
    rows = views.shape[1]
    a, b = views[0].astype(f32), views[1].astype(f32)
    mean_a = jnp.sum(a, 0, keepdims=True) / rows
    mean_b = jnp.sum(b, 0, keepdims=True) / rows
    a, b = a - mean_a, b - mean_b
    moments = (mean_a, mean_b, *(jnp.sum(x, 0, keepdims=True) for x in (a * a, b * b, a * b)))
    for i, value in enumerate(moments):
        for k in range(SUB):
            out[i * SUB + k : i * SUB + k + 1, :] = value[:, k * LANE : (k + 1) * LANE]


def merge(rows, *parts):
    parts = [[p[k * SUB : (k + 1) * SUB, :] for k in range(5)] for p in parts]
    mean_a, mean_b = (sum(p[k] for p in parts) / len(parts) for k in range(2))
    square_a, square_b, product = (sum(p[k] for p in parts) for k in range(2, 5))
    for p in parts:
        gap_a, gap_b = p[0] - mean_a, p[1] - mean_b
        square_a = square_a + rows * gap_a * gap_a
        square_b = square_b + rows * gap_b * gap_b
        product = product + rows * gap_a * gap_b
    return mean_a, mean_b, square_a, square_b, product


def merge_body(rows, *refs):
    *parts, out = refs
    for k, value in enumerate(merge(rows, *parts)):
        out[k * SUB : (k + 1) * SUB, :] = value


def stats_of(batch, moments, stats):
    mean_a, mean_b, square_a, square_b, product = merge(batch // len(moments), *moments)
    spread_a, spread_b = jnp.sqrt(square_a / batch + epsilon), jnp.sqrt(square_b / batch + epsilon)
    corr = product / (batch * spread_a * spread_b)
    diag = 2.0 * (corr - 1.0) - 2.0 * off_weight * corr
    for i, value in enumerate((mean_a, mean_b, spread_a, spread_b, diag)):
        for k in range(SUB):
            stats[i : i + 1, k * LANE : (k + 1) * LANE] = value[k : k + 1, :]


def normal(piece, stats, v):
    return ((piece.astype(f32) - stats[v : v + 1, :]) / stats[2 + v : 3 + v, :]).astype(bf16)


def multiply(lead, pieces, stats, normed, gram):
    rows = pieces[0][0].shape[0]
    for v in range(2):
        for i, piece in enumerate(pieces[v]):
            r = slice(i * rows, (i + 1) * rows)
            normed[v, r, :] = normal(piece[...], stats, v)
            block = lax.dot_general(
                lead[v], normed[v, r, :], (((1,), (1,)), ((), ())), preferred_element_type=f32
            )
            gram[v, :, r] = block.astype(bf16)


def split_views(pairs):
    return [[p.at[v] for p in pairs] for v in range(2)]


def stack_body(a, b, out):
    out[0] = a[...]
    out[1] = b[...]


def copy_body(x, out):
    out[...] = x[...]


def near_body(batch, *refs):
    *moments, sib, views, from_down, from_up, from_x, stats, lead, normed, gram = refs
    pairs = [views, from_down, from_up, from_x]
    rows = sib.shape[1]
    stats_of(batch, moments, stats)
    for v in range(2):
        lead[v, 0:rows, :] = normal(pairs[0][v], stats, v)
        lead[v, rows:, :] = normal(sib[v], stats, v)
    multiply(lead, split_views(pairs), stats, normed, gram)


def last_body(lead, stats, opp_a, opp_b, x_down, x_up, x_far, gram_near, *outs):
    normed, mine, up_2, down_2, up_1, down_1, far_a, far_b, gram = outs
    rows, part = x_far.shape[1], mine.shape[2]
    middle = gram_near.shape[2]
    pieces = split_views([x_down, x_up, x_far])
    multiply(lead, [[opp_a, *pieces[0]], [opp_b, *pieces[1]]], stats, normed, gram)
    z = lax.rem(lax.axis_index("feat"), Z)

    def store(ahead, v, out):
        start = lax.rem(z + ahead, Z) * part
        for h in range(X_HI):
            r = pl.ds(pl.multiple_of(start + h * rows, part), part)
            out[h, :, 0:middle] = gram_near[v, r, :]
            out[h, :, middle:] = gram[v, r, :]

    for v in range(2):
        store(0, v, mine.at[v])
        store(2, v, up_2.at[v])
        store(6, v, down_2.at[v])
        for i, (up, down) in enumerate(((3, 5), (1, 7))):
            store(up, v, up_1.at[i, v])
            store(down, v, down_1.at[i, v])
        store(4, v, (far_a, far_b)[v])


def fold_body(far_up, far_down, half_a, half_b, up_2, down_2, up_out, down_out):
    def plus(x, y, *z):
        total = x.astype(f32) + y.astype(f32)
        return (total + z[0].astype(f32) if z else total).astype(bf16)

    up_out[0] = plus(up_2[0], far_up[0, 0], half_a[...])
    up_out[1] = plus(up_2[1], far_up[0, 1])
    down_out[0] = plus(down_2[0], far_down[0, 0])
    down_out[1] = plus(down_2[1], far_down[0, 1], half_b[...])


def total_body(mine, near_up, near_down, far_up, far_down, out):
    total = mine[...].astype(f32) + near_up[1].astype(f32) + near_down[1].astype(f32)
    out[...] = (total + far_up[...].astype(f32) + far_down[...].astype(f32)).astype(bf16)


def add_body(a, b, out):
    out[...] = (a[...].astype(f32) + b[...].astype(f32)).astype(bf16)


def reduce_rows(mine, up_2, down_2, up_1, down_1, far_a, far_b):
    z = "feat"
    half_a = send(far_a, z_shift(2), z)
    half_b = send(far_b, z_shift(-2), z)
    from_down, from_up = send(up_1, z_shift(1), z), send(down_1, z_shift(-1), z)
    block = jax.ShapeDtypeStruct(mine.shape, bf16)
    up_2, down_2 = call(
        fold_body, (block, block), from_down, from_up, half_a, half_b, up_2, down_2
    )
    far_down, far_up = send(up_2, z_shift(2), z), send(down_2, z_shift(-2), z)
    total = call(total_body, block, mine, from_down, from_up, far_down, far_up)
    return call(add_body, block, total, send(total, TO_X_HI, z))


def spread_rows(block):
    z = "feat"
    from_1 = send(block, z_shift(1), z)
    from_7 = send(block, z_shift(-1), z)
    from_2 = send(block, z_shift(2), z)
    from_6 = send(block, z_shift(-2), z)
    from_3 = send(from_2, z_shift(1), z)
    from_5 = send(from_6, z_shift(-1), z)
    from_4 = send(from_2, z_shift(2), z)
    return [block, from_1, from_2, from_3, from_4, from_5, from_6, from_7]


def apply_body(scale, *refs):
    *blocks, near, last, lead, stats, own, other, sums, gram = refs
    rows, part = own.shape[1], blocks[0].shape[2]
    z = lax.rem(lax.axis_index("feat"), Z)

    def load(back, v, block):
        start = lax.rem(z + Z - back, Z) * part
        for h in range(X_HI):
            gram[v, pl.ds(pl.multiple_of(start + h * rows, part), part), :] = block[h]

    for v in range(2):
        for back, block in enumerate(blocks):
            load(back, v, block.at[v])
    diag = stats[4:5, :]
    ends = (0, near.shape[1], gram.shape[2])
    for v in range(2):
        first = second = 0.0
        for h, out in enumerate((own, other)):
            r = slice(h * rows, (h + 1) * rows)
            up = 0.0
            for i, normed in enumerate((near, last)):
                left = gram[1 - v, r, ends[i] : ends[i + 1]]
                up = up + jnp.dot(left, normed[v], preferred_element_type=f32)
            up = scale * up
            if h == 0:
                up = up + lead[1 - v, r, :].astype(f32) * diag
            out[v] = up
            first = first + jnp.sum(up, 0, keepdims=True)
            second = second + jnp.sum(up * lead[v, r, :].astype(f32), 0, keepdims=True)
        for i in range(sums.shape[0]):
            sums[i, 2 * v : 2 * v + 1, :] = first
            sums[i, 2 * v + 1 : 2 * v + 2, :] = second


def final_body(batch, own, recv, lead, sums, stats, grad_a, grad_b):
    rows = own.shape[1]
    total = sums[0]
    for i in range(1, sums.shape[0]):
        total = total + sums[i]
    total = total / batch
    for v, out in enumerate((grad_a, grad_b)):
        own_normed = lead[v, 0:rows, :].astype(f32)
        first, second = total[2 * v : 2 * v + 1, :], total[2 * v + 1 : 2 * v + 2, :]
        up = own[v] + recv[v]
        out[...] = ((up - first - own_normed * second) / stats[2 + v : 3 + v, :]).astype(bf16)


def on_device(view_a, view_b):
    rows, cols = view_a.shape
    dp_count = lax.axis_size("dp")
    feat_count = lax.axis_size("feat")
    batch = rows * dp_count
    half = batch // CORES
    part = CORES * rows // feat_count
    scale = 2.0 * off_weight / batch
    work = 2 * 2 * CORES * rows * half * cols

    views = jnp.stack([view_a, view_b])
    from_down, from_up, from_x = send(views, TO_UP), send(views, TO_DOWN), send(views, TO_X)
    sib = send(views, TO_CORE)
    tile = shape(5 * SUB, LANE)
    moments = call(moments_body, tile, views)
    moments = call(
        functools.partial(merge_body, rows), tile, moments, send(moments, TO_CORE)
    )
    below, above = send(moments, TO_UP), send(moments, TO_DOWN)
    from_down, from_up, below, above = lax.optimization_barrier((from_down, from_up, below, above))
    opposite = send(below, TO_UP)
    from_x, opposite = lax.optimization_barrier((from_x, opposite))
    moments = call(
        functools.partial(merge_body, CORES * rows), tile, moments, below, above, opposite
    )
    moments_x = send(moments, TO_X)
    far_a, far_b = send(from_down[0], TO_UP), send(from_up[1], TO_DOWN)
    from_x = call(copy_body, jax.ShapeDtypeStruct(from_x.shape, bf16), from_x, flops=10**10)
    x_down, x_up = send(from_x, TO_UP), send(from_x, TO_DOWN)
    far_b, moments_x = lax.optimization_barrier((far_b, moments_x))
    far = call(stack_body, jax.ShapeDtypeStruct(views.shape, bf16), far_a, far_b, flops=10**10)
    x_far = send(far, TO_X)

    def results(pieces):
        return (
            shape(2, pieces * rows, cols, dtype=bf16),
            shape(2, CORES * rows, pieces * rows, dtype=bf16),
        )

    stats, lead, near, gram_near = call(
        functools.partial(near_body, batch),
        (shape(5, cols), shape(2, CORES * rows, cols, dtype=bf16), *results(4)),
        moments,
        moments_x,
        sib,
        views,
        from_down,
        from_up,
        from_x,
        flops=work // 2,
    )
    one = shape(X_HI, part, half, dtype=bf16)
    both = shape(2, *one.shape, dtype=bf16)
    four = shape(2, *both.shape, dtype=bf16)
    last, *chunks = call(
        last_body,
        (results(4)[0], both, both, both, four, four, one, one),
        lead,
        stats,
        far_a,
        far_b,
        x_down,
        x_up,
        x_far,
        gram_near,
        flops=work // 2,
        scratch=[pltpu.VMEM(results(4)[1].shape, bf16)],
    )
    blocks = spread_rows(reduce_rows(*chunks))
    own, other, sums = call(
        functools.partial(apply_body, scale),
        (shape(2, rows, cols), shape(2, rows, cols), shape(dp_count, 4, cols)),
        *blocks,
        near,
        last,
        lead,
        stats,
        flops=work,
        scratch=[pltpu.VMEM((2, CORES * rows, half), bf16)],
    )
    sums = lax.all_to_all(sums, "dp", 0, 0)
    return call(
        functools.partial(final_body, batch),
        (shape(rows, cols, dtype=bf16), shape(rows, cols, dtype=bf16)),
        own,
        send(other, TO_CORE),
        lead,
        sums,
        stats,
    )


def solution(mesh):
    spec = P("dp", "feat")
    return jax.shard_map(
        on_device, mesh=mesh, in_specs=(spec, spec), out_specs=(spec, spec), check_vma=False
    )
```
